128 devices in a mesh: row: 8 (over x_hi, y), col: 16 (over z, x_lo, core).
Axes of the slice: x: 4 (x_hi: 2, x_lo: 2; x = x_hi * 2 + x_lo), y: 4, z: 4, core: 2. Of those that a mesh axis runs over, the one named last changes fastest.
Arguments:
- left_matrix: bfloat16 [32768, 8192], P('row', 'col'), may hold values from -6 to 6
- left_pattern: int32 [256, 64], P('row', 'col'), may hold values from 0 to 1, as said below
- right_matrix: bfloat16 [8192, 16384], P('row', 'col'), may hold values from -0.25 to 0.25
- right_pattern: int32 [64, 128], P('row', 'col'), may hold values from 0 to 1, as said below
- keep_mask: int32 [256, 128], P('row', 'col'), may hold values 0 or 1
Outputs:
- partial_product: bfloat16 [32768, 16384], P('row', 'col')
The draws below stay inside these ranges and needn't reach their ends.
Inputs may be any that keep to these rules, and one draw needn't show every extreme that they name: `left_pattern`: 1 where the block is present; in each aligned tile of 32 block rows by 4 block columns exactly 16 entries are 1. `right_pattern`: 1 where the block is present; in each aligned tile of 4 block rows by 8 block columns exactly 4 entries are 1. `keep_mask`: 1 where the product's block is kept.
All inputs are finite; a program needn't handle non-finite values.
Results may differ from the reference program's by a relative error of at most 0.001.
Values may be sent and summed in bfloat16 or wider, within the bound.
No kernel may reach another device: no remote copies, remote signals or barrier semaphores. Data moves between devices by JAX's collectives and lax.ppermute only.
A program may use at most 192 MiB of HBM per device.

```python
import jax
import jax.numpy as jnp
from jax import lax

BLK = 128
MR = 32
KS = 4
NC = 8
LCAP = 16
RCAP = 4
MB_ALL = 256
KB_ALL = 64
NB_ALL = 128
N_ROW = 8
N_COL = 16


def exact_tiles(key, tiles_r, tiles_c, rows, cols, count):
    keys = jax.random.split(key, tiles_r * tiles_c)
    scores = jax.vmap(lambda k: jax.random.permutation(k, rows * cols))(keys)
    ones = (scores < count).astype(jnp.int32)
    ones = ones.reshape(tiles_r, tiles_c, rows, cols)
    return ones.transpose(0, 2, 1, 3).reshape(tiles_r * rows, tiles_c * cols)


def draw_left_pattern(key, part):
    key = jax.random.fold_in(key, 11)
    return exact_tiles(key, N_ROW, N_COL, MR, KS, LCAP)


def draw_right_pattern(key, part):
    key = jax.random.fold_in(key, 23)
    return exact_tiles(key, N_COL, N_COL, KS, NC, RCAP)


def plant(drawn, stream_key, smallest, largest):
    place = [jax.random.randint(jax.random.fold_in(stream_key, axis), (), 0, length) for axis, length in enumerate(drawn.shape)]
    main_axis = drawn.shape.index(max(drawn.shape))
    beside = place[:main_axis] + [(place[main_axis] + 1) % drawn.shape[main_axis]] + place[main_axis + 1:]
    return drawn.at[tuple(place)].set(smallest).at[tuple(beside)].set(largest)


def steps_of(stream_key, dims, pieces, low, high):
    def one(axis_at, shards_of):
        steps = jax.random.uniform(jax.random.fold_in(jax.random.fold_in(stream_key, 6), axis_at), (shards_of,), jnp.float32, low / len(pieces), high / len(pieces))
        return jnp.repeat(jnp.exp(steps), dims[axis_at] // shards_of).reshape((-1,) + (1,) * (len(dims) - axis_at - 1))

    loudness = one(*pieces[0])
    for cut in pieces[1:]:
        loudness = loudness * one(*cut)
    return loudness


def bell_draw(key, extent, deviation, most, shards=(), held_as=jnp.bfloat16):
    values = deviation * jax.random.normal(key, extent, jnp.float32)
    if shards:
        values = values * steps_of(key, extent, shards, -0.22, 0.18)
    return jnp.clip(values, -most, most).astype(held_as)


def setup_inputs(seed: int = 0) -> dict:
    seeds = jax.random.split(jax.random.key(seed), 6)
    return {
        "left_matrix": bell_draw(seeds[0], (MB_ALL * BLK, KB_ALL * BLK), 1.0, 6.0, ((0, 8), (1, 16))),
        "left_pattern": draw_left_pattern(jax.random.fold_in(seeds[5], 71), 0),
        "right_matrix": bell_draw(seeds[2], (KB_ALL * BLK, NB_ALL * BLK), (KS * BLK) ** -0.5, 0.25, ((0, 8), (1, 16))),
        "right_pattern": draw_right_pattern(jax.random.fold_in(seeds[5], 71), 0),
        "keep_mask": plant((jax.random.randint(seeds[4], (MB_ALL, NB_ALL), 0, 4) < 3).astype(jnp.int32), jax.random.fold_in(seeds[4], 1), 0, 1),
    }


def masked(tile, pattern):
    nrb, ncb = pattern.shape
    side_r = tile.shape[0] // nrb
    side_c = tile.shape[1] // ncb
    shaped = tile.reshape(nrb, side_r, ncb, side_c)
    return (shaped * pattern[:, None, :, None].astype(tile.dtype)).reshape(tile.shape)


def reference(left_matrix, left_pattern, right_matrix, right_pattern, keep_mask):
    group = N_COL // N_ROW

    def one_tile(index):
        row_at = index // N_COL
        col_at = index % N_COL
        total = jnp.zeros((MR * BLK, NC * BLK), jnp.float32)
        for step in range(2):
            seg = (group * row_at + col_at + group * step) % N_COL
            a_part = lax.dynamic_slice(left_matrix, (row_at * MR * BLK, seg * KS * BLK), (MR * BLK, KS * BLK))
            a_mask = lax.dynamic_slice(left_pattern, (row_at * MR, seg * KS), (MR, KS))
            b_part = lax.dynamic_slice(right_matrix, (seg * KS * BLK, col_at * NC * BLK), (KS * BLK, NC * BLK))
            b_mask = lax.dynamic_slice(right_pattern, (seg * KS, col_at * NC), (KS, NC))
            left_f = masked(a_part.astype(jnp.float32), a_mask)
            right_f = masked(b_part.astype(jnp.float32), b_mask)
            total = total + jnp.dot(left_f, right_f, preferred_element_type=jnp.float32, precision=lax.Precision.HIGHEST)
        kept = lax.dynamic_slice(keep_mask, (row_at * MR, col_at * NC), (MR, NC))
        return masked(total, kept).astype(jnp.bfloat16)

    tiles = lax.map(one_tile, jnp.arange(N_ROW * N_COL, dtype=jnp.int32))
    tiles = tiles.reshape(N_ROW, N_COL, MR * BLK, NC * BLK)
    return tiles.transpose(0, 2, 1, 3).reshape(N_ROW * MR * BLK, N_COL * NC * BLK)
```

```python
import functools

import jax
import jax.numpy as jnp
from jax import lax
from jax.experimental import pallas as pl
from jax.experimental.pallas import tpu as pltpu
from jax.sharding import PartitionSpec as P

BLK = 128
MR = 32
KS = 4
NC = 8
LCAP = 16
RCAP = 4
META = 16
LROWS = LCAP * BLK
PAIRS = LCAP * RCAP
TILES = MR * NC
ZROWS = 256


def block_of(ref, block_row, block_col):
    return ref.at[
        pl.ds(pl.multiple_of(block_row * BLK, BLK), BLK),
        pl.ds(pl.multiple_of(block_col * BLK, BLK), BLK),
    ]


def spec(space):
    return pl.BlockSpec(memory_space=space)


def pack_left_kernel(pattern, left, out, pos, meta, sems):
    count = 0
    starts = []
    for k in range(KS):
        starts.append(count)
        for i in range(MR):
            pos[count] = k * MR + i
            count = count + pattern[k, i]
    starts.append(count)
    copies = []
    for a in range(LCAP):
        at = pos[a]
        copies.append(
            pltpu.make_async_copy(
                block_of(left, at & (MR - 1), at >> 5), out.at[pl.ds(a * BLK, BLK), :], sems.at[a]
            )
        )
        copies[-1].start()
    lane = lax.broadcasted_iota(jnp.int32, (META, BLK), 1)
    row = jnp.zeros((META, BLK), jnp.int32)
    for a in range(LCAP):
        row = jnp.where(lane == a, pos[a], row)
    for k in range(KS + 1):
        row = jnp.where(lane == LCAP + k, starts[k], row)
    meta[...] = row.astype(jnp.float32).astype(jnp.bfloat16)
    copies.append(pltpu.make_async_copy(meta, out.at[pl.ds(LROWS, META), :], sems.at[LCAP]))
    copies[-1].start()
    for copy in copies:
        copy.wait()


def pack_left(pattern, left):
    return pl.pallas_call(
        pack_left_kernel,
        out_shape=jax.ShapeDtypeStruct((LROWS + META, BLK), jnp.bfloat16),
        in_specs=[spec(pltpu.SMEM), spec(pltpu.HBM)],
        out_specs=spec(pl.ANY),
        scratch_shapes=[
            pltpu.SMEM((LCAP + 1,), jnp.int32),
            pltpu.VMEM((META, BLK), jnp.bfloat16),
            pltpu.SemaphoreType.DMA((LCAP + 1,)),
        ],
        compiler_params=pltpu.CompilerParams(vmem_limit_bytes=52 << 20),
        cost_estimate=pl.CostEstimate(flops=0, bytes_accessed=2 << 20, transcendentals=0),
        name="pack_left",
    )(pattern.T, left)


def pack_right_kernel(pattern, right, after, out, pos, meta, sems):
    del after
    part = lax.rem(lax.axis_index("col"), 2)
    count = 0
    for k in range(KS):
        for j in range(NC):
            pos[count] = k * NC + j
            count = count + pattern[part * KS + k, j]
    copies = []
    for b in range(RCAP):
        at = pos[b]
        copies.append(
            pltpu.make_async_copy(
                block_of(right, part * KS + (at >> 3), at & (NC - 1)),
                out.at[pl.ds(0, BLK), pl.ds(b * BLK, BLK)],
                sems.at[b],
            )
        )
        copies[-1].start()
    lane = lax.broadcasted_iota(jnp.int32, (META, RCAP * BLK), 1)
    row = jnp.zeros((META, RCAP * BLK), jnp.int32)
    for b in range(RCAP):
        row = jnp.where(lane == b, pos[b], row)
    meta[...] = row.astype(jnp.float32).astype(jnp.bfloat16)
    copies.append(pltpu.make_async_copy(meta, out.at[pl.ds(BLK, META), :], sems.at[RCAP]))
    copies[-1].start()
    for copy in copies:
        copy.wait()


def pack_right(pattern, right, after):
    return pl.pallas_call(
        pack_right_kernel,
        out_shape=jax.ShapeDtypeStruct((BLK + META, RCAP * BLK), jnp.bfloat16),
        in_specs=[spec(pltpu.SMEM), spec(pltpu.HBM), spec(pl.ANY)],
        out_specs=spec(pl.ANY),
        scratch_shapes=[
            pltpu.SMEM((RCAP + 1,), jnp.int32),
            pltpu.VMEM((META, RCAP * BLK), jnp.bfloat16),
            pltpu.SemaphoreType.DMA((RCAP + 1,)),
        ],
        compiler_params=pltpu.CompilerParams(vmem_limit_bytes=52 << 20),
        cost_estimate=pl.CostEstimate(flops=0, bytes_accessed=1 << 20, transcendentals=0),
        name="pack_right",
    )(pattern, right, after)


def piece(code):
    return (
        pl.ds(pl.multiple_of((code >> 2) * BLK, BLK), BLK),
        pl.ds(pl.multiple_of((code & 3) * BLK, BLK), BLK),
    )


def products(left, right, prod):
    chunk = 512
    rhs = right[...]
    for first in range(0, LROWS, chunk):
        rows = pl.ds(first, chunk)
        prod[rows, :] = jnp.dot(left[rows, :], rhs, preferred_element_type=jnp.float32)


def gather(left_at, right_at, kept, owner, prod, slot_of):
    total = 0
    for b in range(RCAP):
        at = right_at(b)
        j = at & (NC - 1)

        def meet(a, total, b=b, j=j):
            target = (left_at(a) & (MR - 1)) * NC + j
            code = a * RCAP + b
            wanted = kept(target)
            held = owner[target]
            fresh = jnp.logical_and(wanted, held == 0)

            @pl.when(fresh)
            def _():
                owner[target] = code + 1
                slot_of[total] = code * TILES + target

            @pl.when(jnp.logical_and(wanted, held != 0))
            def _():
                rows, cols = piece(held - 1)
                more_rows, more_cols = piece(code)
                prod[rows, cols] += prod[more_rows, more_cols]

            return total + fresh.astype(jnp.int32)

        k = at >> 3
        total = lax.fori_loop(left_at(LCAP + k), left_at(LCAP + 1 + k), meet, total)
    return total


def write(total, value, slot_of, stage, out, sems):
    def copy_out(slot, target):
        return pltpu.make_async_copy(
            stage.at[slot], block_of(out, target >> 3, target & (NC - 1)), sems.at[slot]
        )

    def send(slot, carry):
        entry = slot_of[slot]
        target = entry & (TILES - 1)
        stage[slot] = value(entry >> 8, target).astype(jnp.bfloat16)
        copy_out(slot, target).start()
        return carry

    def drain(slot, carry):
        copy_out(slot, slot_of[slot] & (TILES - 1)).wait()
        return carry

    lax.fori_loop(0, total, send, 0)
    lax.fori_loop(0, total, drain, 0)


def choose(flag, first, second, held):
    @pl.when(flag == 0)
    def _():
        held[...] = first[pl.ds(0, BLK), :]

    @pl.when(flag != 0)
    def _():
        held[...] = second[pl.ds(0, BLK), :]


def first_kernel(
    keep, left, r0, r1, out, prod, table,
    zero, zero_sems, right, stage, meta_v, meta, owner, slot_of, meta_sem, out_sems,
):
    zero[...] = jnp.zeros_like(zero)
    clears = [
        pltpu.make_async_copy(zero, out.at[pl.ds(n * ZROWS, ZROWS), :], zero_sems.at[n])
        for n in range(out.shape[0] // ZROWS)
    ]
    for copy in clears:
        copy.start()
    odd = lax.rem(lax.axis_index("row"), 2)
    line = lax.broadcasted_iota(jnp.int32, (META, BLK), 0)
    rows = left[pl.ds(LROWS, META), :].astype(jnp.float32)
    for n, ref in enumerate((r0, r1)):
        more = ref[pl.ds(BLK, META), pl.ds(0, BLK)].astype(jnp.float32)
        rows = jnp.where(line == 1 + n, more, rows)
    meta_v[...] = rows.astype(jnp.int32)
    meta_copy = pltpu.make_async_copy(meta_v, meta, meta_sem)
    meta_copy.start()
    for at in range(TILES):
        owner[at] = 0
    choose(odd, r0, r1, right)
    products(left, right, prod)
    meta_copy.wait()
    total = gather(
        lambda a: meta[0, a],
        lambda b: meta[1 + odd, b],
        lambda target: keep[target >> 3, target & (NC - 1)] != 0,
        owner,
        prod,
        slot_of,
    )

    def value(code, target):
        rows, cols = piece(code)
        return prod[rows, cols]

    for copy in clears:
        copy.wait()
    write(total, value, slot_of, stage, out, out_sems)
    for i in range(MR):
        for j in range(NC):
            table[i * NC + j] = jnp.where(keep[i, j] != 0, owner[i * NC + j], -1)
    for b in range(RCAP):
        table[TILES + b] = meta[2 - odd, b]


def first(keep, left, r0, r1):
    return pl.pallas_call(
        first_kernel,
        out_shape=(
            jax.ShapeDtypeStruct((MR * BLK, NC * BLK), jnp.bfloat16),
            jax.ShapeDtypeStruct((LROWS, RCAP * BLK), jnp.float32),
            jax.ShapeDtypeStruct((TILES + BLK,), jnp.int32),
        ),
        in_specs=[spec(pltpu.SMEM)] + [spec(pltpu.VMEM)] * 3,
        out_specs=[spec(pltpu.HBM), spec(pltpu.VMEM), spec(pltpu.SMEM)],
        scratch_shapes=[
            pltpu.VMEM((ZROWS, NC * BLK), jnp.bfloat16),
            pltpu.SemaphoreType.DMA((MR * BLK // ZROWS,)),
            pltpu.VMEM((BLK, RCAP * BLK), jnp.bfloat16),
            pltpu.VMEM((PAIRS, BLK, BLK), jnp.bfloat16),
            pltpu.VMEM((META, BLK), jnp.int32),
            pltpu.SMEM((META, BLK), jnp.int32),
            pltpu.SMEM((TILES,), jnp.int32),
            pltpu.SMEM((PAIRS,), jnp.int32),
            pltpu.SemaphoreType.DMA,
            pltpu.SemaphoreType.DMA((PAIRS,)),
        ],
        compiler_params=pltpu.CompilerParams(vmem_limit_bytes=32 << 20),
        cost_estimate=pl.CostEstimate(
            flops=10**10, bytes_accessed=14 << 20, transcendentals=0
        ),
        name="first",
    )(keep, left, r0, r1)


def last_kernel(
    table, left, r0, r1, before, zero, out,
    right, prod, stage, meta_v, meta, owner, slot_of, meta_sem, out_sems,
):
    del zero
    odd = lax.rem(lax.axis_index("row"), 2)
    meta_v[...] = left[pl.ds(LROWS, META), :].astype(jnp.float32).astype(jnp.int32)
    meta_copy = pltpu.make_async_copy(meta_v, meta, meta_sem)
    meta_copy.start()
    for at in range(TILES):
        owner[at] = 0
    choose(odd, r1, r0, right)
    products(left, right, prod)
    meta_copy.wait()
    total = gather(
        lambda a: meta[0, a],
        lambda b: table[TILES + b],
        lambda target: table[target] >= 0,
        owner,
        prod,
        slot_of,
    )

    def value(code, target):
        rows, cols = piece(code)
        held = table[target]
        old_rows, old_cols = piece(jnp.maximum(held - 1, 0))
        fresh = prod[rows, cols]
        return jnp.where(held > 0, fresh + before[old_rows, old_cols], fresh)

    write(total, value, slot_of, stage, out, out_sems)


def last(table, left, r0, r1, before, out):
    return pl.pallas_call(
        last_kernel,
        out_shape=jax.ShapeDtypeStruct(out.shape, out.dtype),
        in_specs=[spec(pltpu.SMEM)] + [spec(pltpu.VMEM)] * 4 + [spec(pltpu.HBM)],
        out_specs=spec(pltpu.HBM),
        scratch_shapes=[
            pltpu.VMEM((BLK, RCAP * BLK), jnp.bfloat16),
            pltpu.VMEM((LROWS, RCAP * BLK), jnp.float32),
            pltpu.VMEM((PAIRS, BLK, BLK), jnp.bfloat16),
            pltpu.VMEM((META, BLK), jnp.int32),
            pltpu.SMEM((META, BLK), jnp.int32),
            pltpu.SMEM((TILES,), jnp.int32),
            pltpu.SMEM((PAIRS,), jnp.int32),
            pltpu.SemaphoreType.DMA,
            pltpu.SemaphoreType.DMA((PAIRS,)),
        ],
        input_output_aliases={5: 0},
        compiler_params=pltpu.CompilerParams(vmem_limit_bytes=32 << 20),
        cost_estimate=pl.CostEstimate(
            flops=2 * PAIRS * BLK**3, bytes_accessed=4 << 20, transcendentals=0
        ),
        name="last",
    )(table, left, r0, r1, before, out)


def on_device(rows_n, cols_n, left_matrix, left_pattern, right_matrix, right_pattern, keep_mask):
    group = cols_n // rows_n

    def moved(value, target):
        pairs = []
        for r in range(rows_n):
            for c in range(cols_n):
                to_r, to_c = target(r, c)
                pairs.append((r * cols_n + c, to_r % rows_n * cols_n + to_c % cols_n))
        return lax.ppermute(value, ("row", "col"), pairs)

    lpack = pack_left(left_pattern, left_matrix)
    even = moved(lpack, lambda r, c: (r, c - group * (r + r % 2)))
    rpack = pack_right(right_pattern, right_matrix, lpack)
    r0 = moved(rpack, lambda r, c: (r - c // group, c))
    r1 = moved(rpack, lambda r, c: (r - c // group - 1, c))
    other = moved(even, lambda r, c: (r, c + group * (2 * (r % 2) - 1)))
    out, before, table = first(keep_mask, even, r0, r1)
    return last(table, other, r0, r1, before, out)


def solution(mesh):
    part = P("row", "col")
    return jax.shard_map(
        functools.partial(on_device, mesh.shape["row"], mesh.shape["col"]),
        mesh=mesh,
        in_specs=(part,) * 5,
        out_specs=part,
        check_vma=False,
    )
```

```python
import functools

import jax
import jax.numpy as jnp
from jax import lax
from jax.experimental import pallas as pl
from jax.experimental.pallas import tpu as pltpu
from jax.sharding import PartitionSpec as P

BLK = 128
MR = 32
KS = 4
NC = 8
LCAP = 16
RCAP = 4
META = 16
LROWS = LCAP * BLK
HALF = LROWS // 2
PAIRS = LCAP * RCAP
TILES = MR * NC
ZROWS = 256


def block_of(ref, block_row, block_col):
    return ref.at[
        pl.ds(pl.multiple_of(block_row * BLK, BLK), BLK),
        pl.ds(pl.multiple_of(block_col * BLK, BLK), BLK),
    ]


def spec(space):
    return pl.BlockSpec(memory_space=space)


def pack_left_kernel(pattern, left, out, more, pos, meta, sems):
    count = 0
    starts = []
    for k in range(KS):
        starts.append(count)
        for i in range(MR):
            pos[count] = k * MR + i
            count = count + pattern[k, i]
    starts.append(count)
    copies = []
    for a in range(LCAP):
        at = pos[a]
        block = block_of(left, at & (MR - 1), at >> 5)
        first_row = a * BLK if a * BLK < HALF else a * BLK + META
        copies.append(pltpu.make_async_copy(block, out.at[pl.ds(first_row, BLK), :], sems.at[a]))
        copies[-1].start()
        if a * BLK >= HALF:
            copies.append(
                pltpu.make_async_copy(
                    block, more.at[pl.ds(a * BLK - HALF, BLK), :], sems.at[LCAP + a - LCAP // 2]
                )
            )
            copies[-1].start()
    lane = lax.broadcasted_iota(jnp.int32, (META, BLK), 1)
    row = jnp.zeros((META, BLK), jnp.int32)
    for a in range(LCAP):
        row = jnp.where(lane == a, pos[a], row)
    for k in range(KS + 1):
        row = jnp.where(lane == LCAP + k, starts[k], row)
    meta[...] = row.astype(jnp.float32).astype(jnp.bfloat16)
    copies.append(pltpu.make_async_copy(meta, out.at[pl.ds(HALF, META), :], sems.at[LCAP + LCAP // 2]))
    copies[-1].start()
    for copy in copies:
        copy.wait()


def pack_left(pattern, left):
    return pl.pallas_call(
        pack_left_kernel,
        out_shape=(
            jax.ShapeDtypeStruct((LROWS + META, BLK), jnp.bfloat16),
            jax.ShapeDtypeStruct((HALF, BLK), jnp.bfloat16),
        ),
        in_specs=[spec(pltpu.SMEM), spec(pltpu.HBM)],
        out_specs=[spec(pl.ANY)] * 2,
        scratch_shapes=[
            pltpu.SMEM((LCAP + 1,), jnp.int32),
            pltpu.VMEM((META, BLK), jnp.bfloat16),
            pltpu.SemaphoreType.DMA((LCAP + LCAP // 2 + 1,)),
        ],
        compiler_params=pltpu.CompilerParams(vmem_limit_bytes=52 << 20),
        cost_estimate=pl.CostEstimate(flops=0, bytes_accessed=2 << 20, transcendentals=0),
        name="pack_left",
    )(pattern.T, left)


def pack_right_kernel(pattern, right, after, out, pos, meta, sems):
    del after
    part = lax.rem(lax.axis_index("col"), 2)
    count = 0
    for k in range(KS):
        for j in range(NC):
            pos[count] = k * NC + j
            count = count + pattern[part * KS + k, j]
    copies = []
    for b in range(RCAP):
        at = pos[b]
        copies.append(
            pltpu.make_async_copy(
                block_of(right, part * KS + (at >> 3), at & (NC - 1)),
                out.at[pl.ds(0, BLK), pl.ds(b * BLK, BLK)],
                sems.at[b],
            )
        )
        copies[-1].start()
    lane = lax.broadcasted_iota(jnp.int32, (META, RCAP * BLK), 1)
    row = jnp.zeros((META, RCAP * BLK), jnp.int32)
    for b in range(RCAP):
        row = jnp.where(lane == b, pos[b], row)
    meta[...] = row.astype(jnp.float32).astype(jnp.bfloat16)
    copies.append(pltpu.make_async_copy(meta, out.at[pl.ds(BLK, META), :], sems.at[RCAP]))
    copies[-1].start()
    for copy in copies:
        copy.wait()


def pack_right(pattern, right, after):
    return pl.pallas_call(
        pack_right_kernel,
        out_shape=jax.ShapeDtypeStruct((BLK + META, RCAP * BLK), jnp.bfloat16),
        in_specs=[spec(pltpu.SMEM), spec(pltpu.HBM), spec(pl.ANY)],
        out_specs=spec(pl.ANY),
        scratch_shapes=[
            pltpu.SMEM((RCAP + 1,), jnp.int32),
            pltpu.VMEM((META, RCAP * BLK), jnp.bfloat16),
            pltpu.SemaphoreType.DMA((RCAP + 1,)),
        ],
        compiler_params=pltpu.CompilerParams(vmem_limit_bytes=52 << 20),
        cost_estimate=pl.CostEstimate(flops=0, bytes_accessed=1 << 20, transcendentals=0),
        name="pack_right",
    )(pattern, right, after)


def piece(code):
    return (
        pl.ds(pl.multiple_of((code >> 2) * BLK, BLK), BLK),
        pl.ds(pl.multiple_of((code & 3) * BLK, BLK), BLK),
    )


def products(halves, right, prod):
    chunk = 512
    rhs = right[...]
    for n, (ref, begin) in enumerate(halves):
        for first in range(0, HALF, chunk):
            prod[pl.ds(n * HALF + first, chunk), :] = jnp.dot(
                ref[pl.ds(begin + first, chunk), :], rhs, preferred_element_type=jnp.float32
            )


def gather(left_at, right_at, kept, owner, prod, slot_of):
    total = 0
    for b in range(RCAP):
        at = right_at(b)
        j = at & (NC - 1)

        def meet(a, total, b=b, j=j):
            target = (left_at(a) & (MR - 1)) * NC + j
            code = a * RCAP + b
            wanted = kept(target)
            held = owner[target]
            fresh = jnp.logical_and(wanted, held == 0)

            @pl.when(fresh)
            def _():
                owner[target] = code + 1
                slot_of[total] = code * TILES + target

            @pl.when(jnp.logical_and(wanted, held != 0))
            def _():
                rows, cols = piece(held - 1)
                more_rows, more_cols = piece(code)
                prod[rows, cols] += prod[more_rows, more_cols]

            return total + fresh.astype(jnp.int32)

        k = at >> 3
        total = lax.fori_loop(left_at(LCAP + k), left_at(LCAP + 1 + k), meet, total)
    return total


def write(total, value, slot_of, stage, out, sems):
    def copy_out(slot, target):
        return pltpu.make_async_copy(
            stage.at[slot], block_of(out, target >> 3, target & (NC - 1)), sems.at[slot]
        )

    def send(slot, carry):
        entry = slot_of[slot]
        target = entry & (TILES - 1)
        stage[slot] = value(entry >> 8, target).astype(jnp.bfloat16)
        copy_out(slot, target).start()
        return carry

    def drain(slot, carry):
        copy_out(slot, slot_of[slot] & (TILES - 1)).wait()
        return carry

    lax.fori_loop(0, total, send, 0)
    lax.fori_loop(0, total, drain, 0)


def choose(flag, first, second, held):
    @pl.when(flag == 0)
    def _():
        held[...] = first[pl.ds(0, BLK), :]

    @pl.when(flag != 0)
    def _():
        held[...] = second[pl.ds(0, BLK), :]


def first_kernel(
    keep, left, r0, r1, out, prod, table,
    zero, zero_sems, right, stage, meta_v, meta, owner, slot_of, meta_sem, out_sems,
):
    zero[...] = jnp.zeros_like(zero)
    clears = [
        pltpu.make_async_copy(zero, out.at[pl.ds(n * ZROWS, ZROWS), :], zero_sems.at[n])
        for n in range(out.shape[0] // ZROWS)
    ]
    for copy in clears:
        copy.start()
    odd = lax.rem(lax.axis_index("row"), 2)
    line = lax.broadcasted_iota(jnp.int32, (META, BLK), 0)
    rows = left[pl.ds(HALF, META), :].astype(jnp.float32)
    for n, ref in enumerate((r0, r1)):
        right_row = ref[pl.ds(BLK, META), pl.ds(0, BLK)].astype(jnp.float32)
        rows = jnp.where(line == 1 + n, right_row, rows)
    meta_v[...] = rows.astype(jnp.int32)
    meta_copy = pltpu.make_async_copy(meta_v, meta, meta_sem)
    meta_copy.start()
    for at in range(TILES):
        owner[at] = 0
    choose(odd, r0, r1, right)
    products(((left, 0), (left, HALF + META)), right, prod)
    meta_copy.wait()
    total = gather(
        lambda a: meta[0, a],
        lambda b: meta[1 + odd, b],
        lambda target: keep[target >> 3, target & (NC - 1)] != 0,
        owner,
        prod,
        slot_of,
    )

    def value(code, target):
        rows, cols = piece(code)
        return prod[rows, cols]

    for copy in clears:
        copy.wait()
    write(total, value, slot_of, stage, out, out_sems)
    for i in range(MR):
        for j in range(NC):
            table[i * NC + j] = jnp.where(keep[i, j] != 0, owner[i * NC + j], -1)
    for b in range(RCAP):
        table[TILES + b] = meta[2 - odd, b]


def first(keep, left, r0, r1):
    return pl.pallas_call(
        first_kernel,
        out_shape=(
            jax.ShapeDtypeStruct((MR * BLK, NC * BLK), jnp.bfloat16),
            jax.ShapeDtypeStruct((LROWS, RCAP * BLK), jnp.float32),
            jax.ShapeDtypeStruct((TILES + BLK,), jnp.int32),
        ),
        in_specs=[spec(pltpu.SMEM)] + [spec(pltpu.VMEM)] * 3,
        out_specs=[spec(pltpu.HBM), spec(pltpu.VMEM), spec(pltpu.SMEM)],
        scratch_shapes=[
            pltpu.VMEM((ZROWS, NC * BLK), jnp.bfloat16),
            pltpu.SemaphoreType.DMA((MR * BLK // ZROWS,)),
            pltpu.VMEM((BLK, RCAP * BLK), jnp.bfloat16),
            pltpu.VMEM((PAIRS, BLK, BLK), jnp.bfloat16),
            pltpu.VMEM((META, BLK), jnp.int32),
            pltpu.SMEM((META, BLK), jnp.int32),
            pltpu.SMEM((TILES,), jnp.int32),
            pltpu.SMEM((PAIRS,), jnp.int32),
            pltpu.SemaphoreType.DMA,
            pltpu.SemaphoreType.DMA((PAIRS,)),
        ],
        compiler_params=pltpu.CompilerParams(vmem_limit_bytes=32 << 20),
        cost_estimate=pl.CostEstimate(
            flops=10**10, bytes_accessed=14 << 20, transcendentals=0
        ),
        name="first",
    )(keep, left, r0, r1)


def last_kernel(
    table, left, more, r0, r1, before, zero, out,
    right, prod, stage, meta_v, meta, owner, slot_of, meta_sem, out_sems,
):
    del zero
    odd = lax.rem(lax.axis_index("row"), 2)
    meta_v[...] = left[pl.ds(HALF, META), :].astype(jnp.float32).astype(jnp.int32)
    meta_copy = pltpu.make_async_copy(meta_v, meta, meta_sem)
    meta_copy.start()
    for at in range(TILES):
        owner[at] = 0
    choose(odd, r1, r0, right)
    products(((left, 0), (more, 0)), right, prod)
    meta_copy.wait()
    total = gather(
        lambda a: meta[0, a],
        lambda b: table[TILES + b],
        lambda target: table[target] >= 0,
        owner,
        prod,
        slot_of,
    )

    def value(code, target):
        rows, cols = piece(code)
        held = table[target]
        old_rows, old_cols = piece(jnp.maximum(held - 1, 0))
        fresh = prod[rows, cols]
        return jnp.where(held > 0, fresh + before[old_rows, old_cols], fresh)

    write(total, value, slot_of, stage, out, out_sems)


def last(table, left, more, r0, r1, before, out):
    return pl.pallas_call(
        last_kernel,
        out_shape=jax.ShapeDtypeStruct(out.shape, out.dtype),
        in_specs=[spec(pltpu.SMEM)] + [spec(pltpu.VMEM)] * 5 + [spec(pltpu.HBM)],
        out_specs=spec(pltpu.HBM),
        scratch_shapes=[
            pltpu.VMEM((BLK, RCAP * BLK), jnp.bfloat16),
            pltpu.VMEM((LROWS, RCAP * BLK), jnp.float32),
            pltpu.VMEM((PAIRS, BLK, BLK), jnp.bfloat16),
            pltpu.VMEM((META, BLK), jnp.int32),
            pltpu.SMEM((META, BLK), jnp.int32),
            pltpu.SMEM((TILES,), jnp.int32),
            pltpu.SMEM((PAIRS,), jnp.int32),
            pltpu.SemaphoreType.DMA,
            pltpu.SemaphoreType.DMA((PAIRS,)),
        ],
        input_output_aliases={6: 0},
        compiler_params=pltpu.CompilerParams(vmem_limit_bytes=32 << 20),
        cost_estimate=pl.CostEstimate(
            flops=2 * PAIRS * BLK**3, bytes_accessed=4 << 20, transcendentals=0
        ),
        name="last",
    )(table, left, more, r0, r1, before, out)


def detour(r, c, cols_n, group):
    core, chip = c % group, c // group
    z, x = chip // 2, chip % 2
    depth = cols_n // group // 2
    step = (r + r % 2) // 2 % depth
    source = (chip + r + 1 - r % 2) % (cols_n // group)
    place = source // 2
    if step == 0:
        place = z
    elif 2 * step != depth and 2 * (place - z) % (2 * depth) == depth:
        place = (place + step) % depth
    return source * group + core, (place * 2 + x) * group + core


def on_device(rows_n, cols_n, left_matrix, left_pattern, right_matrix, right_pattern, keep_mask):
    group = cols_n // rows_n

    def send(value, pairs):
        pairs = [(a[0] * cols_n + a[1], b[0] * cols_n + b[1]) for a, b in pairs]
        return lax.ppermute(value, ("row", "col"), pairs)

    devices = [(r, c) for r in range(rows_n) for c in range(cols_n)]

    def moved(value, target):
        pairs = []
        for r, c in devices:
            to_r, to_c = target(r, c)
            pairs.append(((r, c), (to_r % rows_n, to_c % cols_n)))
        return send(value, pairs)

    whole, half = pack_left(left_pattern, left_matrix)
    even = moved(whole, lambda r, c: (r, c - group * (r + r % 2)))
    roads = {at: detour(*at, cols_n, group) for at in devices}
    between = send(half, [((r, roads[r, c][0]), (r, roads[r, c][1])) for r, c in devices])
    rpack = pack_right(right_pattern, right_matrix, whole)
    r0 = moved(rpack, lambda r, c: (r - c // group, c))
    r1 = moved(rpack, lambda r, c: (r - c // group - 1, c))
    passed = moved(
        lax.slice_in_dim(even, 0, HALF + META),
        lambda r, c: (r, c + group * (2 * (r % 2) - 1)),
    )
    more = send(between, [((r, roads[r, c][1]), (r, c)) for r, c in devices])
    out, before, table = first(keep_mask, even, r0, r1)
    return last(table, passed, more, r0, r1, before, out)


def solution(mesh):
    part = P("row", "col")
    return jax.shard_map(
        functools.partial(on_device, mesh.shape["row"], mesh.shape["col"]),
        mesh=mesh,
        in_specs=(part,) * 5,
        out_specs=part,
        check_vma=False,
    )
```

```python
import functools

import jax
import jax.numpy as jnp
from jax import lax
from jax.experimental import pallas as pl
from jax.experimental.pallas import tpu as pltpu
from jax.sharding import PartitionSpec as P

BLK = 128
MR = 32
KS = 4
NC = 8
LCAP = 16
RCAP = 4
META = 16
LROWS = LCAP * BLK
HALF = LROWS // 2
PAIRS = LCAP * RCAP
TILES = MR * NC


def block_of(ref, block_row, block_col):
    return ref.at[
        pl.ds(pl.multiple_of(block_row * BLK, BLK), BLK),
        pl.ds(pl.multiple_of(block_col * BLK, BLK), BLK),
    ]


def spec(space):
    return pl.BlockSpec(memory_space=space)


def pack_kernel(lpat, rpat, left, right, lout, rout, lpos, rpos, lmeta, rmeta, sems, rsems):
    part = lax.rem(lax.axis_index("col"), 2)
    count = 0
    starts = []
    for k in range(KS):
        starts.append(count)
        for i in range(MR):
            lpos[count] = k * MR + i
            count = count + lpat[k, i]
    starts.append(count)
    copies = []
    for a in range(LCAP):
        at = lpos[a]
        first_row = a * BLK if a * BLK < HALF else a * BLK + META
        copies.append(
            pltpu.make_async_copy(
                block_of(left, at & (MR - 1), at >> 5), lout.at[pl.ds(first_row, BLK), :], sems.at[a]
            )
        )
        copies[-1].start()
    count = 0
    for k in range(KS):
        for j in range(NC):
            rpos[count] = k * NC + j
            count = count + rpat[part * KS + k, j]
    for b in range(RCAP):
        at = rpos[b]
        copies.append(
            pltpu.make_async_copy(
                block_of(right, part * KS + (at >> 3), at & (NC - 1)),
                rout.at[pl.ds(0, BLK), pl.ds(b * BLK, BLK)],
                rsems.at[b],
            )
        )
        copies[-1].start()
    lane = lax.broadcasted_iota(jnp.int32, (META, BLK), 1)
    row = jnp.zeros((META, BLK), jnp.int32)
    for a in range(LCAP):
        row = jnp.where(lane == a, lpos[a], row)
    for k in range(KS + 1):
        row = jnp.where(lane == LCAP + k, starts[k], row)
    lmeta[...] = row.astype(jnp.float32).astype(jnp.bfloat16)
    copies.append(pltpu.make_async_copy(lmeta, lout.at[pl.ds(HALF, META), :], sems.at[LCAP]))
    copies[-1].start()
    lane = lax.broadcasted_iota(jnp.int32, (META, RCAP * BLK), 1)
    row = jnp.zeros((META, RCAP * BLK), jnp.int32)
    for b in range(RCAP):
        row = jnp.where(lane == b, rpos[b], row)
    rmeta[...] = row.astype(jnp.float32).astype(jnp.bfloat16)
    copies.append(pltpu.make_async_copy(rmeta, rout.at[pl.ds(BLK, META), :], rsems.at[RCAP]))
    copies[-1].start()
    for copy in copies:
        copy.wait()


def pack(left_pattern, right_pattern, left, right):
    return pl.pallas_call(
        pack_kernel,
        out_shape=(
            jax.ShapeDtypeStruct((LROWS + META, BLK), jnp.bfloat16),
            jax.ShapeDtypeStruct((BLK + META, RCAP * BLK), jnp.bfloat16),
        ),
        in_specs=[spec(pltpu.SMEM), spec(pltpu.SMEM), spec(pltpu.HBM), spec(pltpu.HBM)],
        out_specs=[spec(pl.ANY)] * 2,
        scratch_shapes=[
            pltpu.SMEM((LCAP + 1,), jnp.int32),
            pltpu.SMEM((RCAP + 1,), jnp.int32),
            pltpu.VMEM((META, BLK), jnp.bfloat16),
            pltpu.VMEM((META, RCAP * BLK), jnp.bfloat16),
            pltpu.SemaphoreType.DMA((LCAP + 1,)),
            pltpu.SemaphoreType.DMA((RCAP + 1,)),
        ],
        compiler_params=pltpu.CompilerParams(vmem_limit_bytes=52 << 20),
        cost_estimate=pl.CostEstimate(flops=0, bytes_accessed=2 << 20, transcendentals=0),
        name="pack",
    )(left_pattern.T, right_pattern, left, right)


def second_half_kernel(whole, after, half):
    del after
    half[...] = whole[pl.ds(HALF + META, HALF), :]


def second_half(whole, after):
    return pl.pallas_call(
        second_half_kernel,
        out_shape=jax.ShapeDtypeStruct((HALF, BLK), jnp.bfloat16),
        in_specs=[spec(pltpu.VMEM), spec(pl.ANY)],
        out_specs=spec(pltpu.VMEM),
        cost_estimate=pl.CostEstimate(flops=0, bytes_accessed=1 << 19, transcendentals=0),
        name="second_half",
    )(whole, after)


def blank_kernel(after, out, zero, sems):
    del after
    zero[...] = jnp.zeros_like(zero)
    rows = zero.shape[0]
    copies = [
        pltpu.make_async_copy(zero, out.at[pl.ds(n * rows, rows), :], sems.at[n])
        for n in range(out.shape[0] // rows)
    ]
    for copy in copies:
        copy.start()
    for copy in copies:
        copy.wait()


def blank(after, shape):
    rows = 256
    return pl.pallas_call(
        blank_kernel,
        out_shape=jax.ShapeDtypeStruct(shape, jnp.bfloat16),
        in_specs=[spec(pl.ANY)],
        out_specs=spec(pltpu.HBM),
        scratch_shapes=[
            pltpu.VMEM((rows, shape[1]), jnp.bfloat16),
            pltpu.SemaphoreType.DMA((shape[0] // rows,)),
        ],
        cost_estimate=pl.CostEstimate(
            flops=0, bytes_accessed=2 * shape[0] * shape[1], transcendentals=0
        ),
        name="blank",
    )(after)


def piece(code):
    return (
        pl.ds(pl.multiple_of((code >> 2) * BLK, BLK), BLK),
        pl.ds(pl.multiple_of((code & 3) * BLK, BLK), BLK),
    )


def products(halves, right, prod):
    chunk = 512
    rhs = right[...]
    for n, (ref, begin) in enumerate(halves):
        for first in range(0, HALF, chunk):
            prod[pl.ds(n * HALF + first, chunk), :] = jnp.dot(
                ref[pl.ds(begin + first, chunk), :], rhs, preferred_element_type=jnp.float32
            )


def gather(left_at, right_at, kept, owner, prod, slot_of):
    total = 0
    for b in range(RCAP):
        at = right_at(b)
        j = at & (NC - 1)

        def meet(a, total, b=b, j=j):
            target = (left_at(a) & (MR - 1)) * NC + j
            code = a * RCAP + b
            wanted = kept[target] >= 0
            held = owner[target]
            fresh = jnp.logical_and(wanted, held == 0)

            @pl.when(fresh)
            def _():
                owner[target] = code + 1
                slot_of[total] = code * TILES + target

            @pl.when(jnp.logical_and(wanted, held > 0))
            def _():
                rows, cols = piece(held - 1)
                more_rows, more_cols = piece(code)
                prod[rows, cols] += prod[more_rows, more_cols]

            return total + fresh.astype(jnp.int32)

        k = at >> 3
        total = lax.fori_loop(left_at(LCAP + k), left_at(LCAP + 1 + k), meet, total)
    return total


def write(total, value, slot_of, stage, out, sems):
    def copy_out(slot, target):
        return pltpu.make_async_copy(
            stage.at[slot], block_of(out, target >> 3, target & (NC - 1)), sems.at[slot]
        )

    def send(slot, carry):
        entry = slot_of[slot]
        target = entry & (TILES - 1)
        stage[slot] = value(entry >> 8, target).astype(jnp.bfloat16)
        copy_out(slot, target).start()
        return carry

    def drain(slot, carry):
        copy_out(slot, slot_of[slot] & (TILES - 1)).wait()
        return carry

    lax.fori_loop(0, total, send, 0)
    lax.fori_loop(0, total, drain, 0)


def choose(flag, first, second, held):
    @pl.when(flag == 0)
    def _():
        held[...] = first[pl.ds(0, BLK), :]

    @pl.when(flag != 0)
    def _():
        held[...] = second[pl.ds(0, BLK), :]


def first_kernel(
    keep, left, r0, r1, zero, out, prod, table,
    right, stage, meta_v, meta, slot_of, meta_sem, out_sems,
):
    del zero
    odd = lax.rem(lax.axis_index("row"), 2)
    line = lax.broadcasted_iota(jnp.int32, (META, BLK), 0)
    rows = left[pl.ds(HALF, META), :].astype(jnp.float32)
    for n, ref in enumerate((r0, r1)):
        right_row = ref[pl.ds(BLK, META), pl.ds(0, BLK)].astype(jnp.float32)
        rows = jnp.where(line == 1 + n, right_row, rows)
    meta_v[...] = rows.astype(jnp.int32)
    meta_copy = pltpu.make_async_copy(meta_v, meta, meta_sem)
    meta_copy.start()
    for at in range(TILES):
        table[at] = jnp.minimum(keep[at // NC, at % NC], 1) - 1
    choose(odd, r0, r1, right)
    products(((left, 0), (left, HALF + META)), right, prod)
    meta_copy.wait()
    total = gather(
        lambda a: meta[0, a],
        lambda b: meta[1 + odd, b],
        table,
        table,
        prod,
        slot_of,
    )

    def value(code, target):
        rows, cols = piece(code)
        return prod[rows, cols]

    write(total, value, slot_of, stage, out, out_sems)
    for b in range(RCAP):
        table[TILES + b] = meta[2 - odd, b]


def first(keep, left, r0, r1, zero):
    return pl.pallas_call(
        first_kernel,
        out_shape=(
            jax.ShapeDtypeStruct(zero.shape, zero.dtype),
            jax.ShapeDtypeStruct((LROWS, RCAP * BLK), jnp.float32),
            jax.ShapeDtypeStruct((TILES + BLK,), jnp.int32),
        ),
        in_specs=[spec(pltpu.SMEM)] + [spec(pltpu.VMEM)] * 3 + [spec(pltpu.HBM)],
        out_specs=[spec(pltpu.HBM), spec(pltpu.VMEM), spec(pltpu.SMEM)],
        scratch_shapes=[
            pltpu.VMEM((BLK, RCAP * BLK), jnp.bfloat16),
            pltpu.VMEM((PAIRS, BLK, BLK), jnp.bfloat16),
            pltpu.VMEM((META, BLK), jnp.int32),
            pltpu.SMEM((META, BLK), jnp.int32),
            pltpu.SMEM((PAIRS,), jnp.int32),
            pltpu.SemaphoreType.DMA,
            pltpu.SemaphoreType.DMA((PAIRS,)),
        ],
        input_output_aliases={4: 0},
        compiler_params=pltpu.CompilerParams(vmem_limit_bytes=32 << 20),
        cost_estimate=pl.CostEstimate(
            flops=10**10, bytes_accessed=14 << 20, transcendentals=0
        ),
        name="first",
    )(keep, left, r0, r1, zero)


def last_kernel(
    table, left, more, r0, r1, before, zero, out,
    right, prod, stage, meta_v, meta, owner, slot_of, meta_sem, out_sems,
):
    del zero
    odd = lax.rem(lax.axis_index("row"), 2)
    meta_v[...] = left[pl.ds(HALF, META), :].astype(jnp.float32).astype(jnp.int32)
    meta_copy = pltpu.make_async_copy(meta_v, meta, meta_sem)
    meta_copy.start()
    for at in range(TILES):
        owner[at] = 0
    choose(odd, r1, r0, right)
    products(((left, 0), (more, 0)), right, prod)
    meta_copy.wait()
    total = gather(
        lambda a: meta[0, a],
        lambda b: table[TILES + b],
        table,
        owner,
        prod,
        slot_of,
    )

    def value(code, target):
        rows, cols = piece(code)
        held = table[target]
        old_rows, old_cols = piece(jnp.maximum(held - 1, 0))
        fresh = prod[rows, cols]
        return jnp.where(held > 0, fresh + before[old_rows, old_cols], fresh)

    write(total, value, slot_of, stage, out, out_sems)


def last(table, left, more, r0, r1, before, out):
    return pl.pallas_call(
        last_kernel,
        out_shape=jax.ShapeDtypeStruct(out.shape, out.dtype),
        in_specs=[spec(pltpu.SMEM)] + [spec(pltpu.VMEM)] * 5 + [spec(pltpu.HBM)],
        out_specs=spec(pltpu.HBM),
        scratch_shapes=[
            pltpu.VMEM((BLK, RCAP * BLK), jnp.bfloat16),
            pltpu.VMEM((LROWS, RCAP * BLK), jnp.float32),
            pltpu.VMEM((PAIRS, BLK, BLK), jnp.bfloat16),
            pltpu.VMEM((META, BLK), jnp.int32),
            pltpu.SMEM((META, BLK), jnp.int32),
            pltpu.SMEM((TILES,), jnp.int32),
            pltpu.SMEM((PAIRS,), jnp.int32),
            pltpu.SemaphoreType.DMA,
            pltpu.SemaphoreType.DMA((PAIRS,)),
        ],
        input_output_aliases={6: 0},
        compiler_params=pltpu.CompilerParams(vmem_limit_bytes=32 << 20),
        cost_estimate=pl.CostEstimate(
            flops=2 * PAIRS * BLK**3, bytes_accessed=4 << 20, transcendentals=0
        ),
        name="last",
    )(table, left, more, r0, r1, before, out)


def detour(r, c, cols_n, group):
    core, chip = c % group, c // group
    z, x = chip // 2, chip % 2
    depth = cols_n // group // 2
    step = (r + r % 2) // 2 % depth
    source = (chip + r + 1 - r % 2) % (cols_n // group)
    place = source // 2
    if step == 0:
        place = z
    elif 2 * step != depth and 2 * (place - z) % (2 * depth) == depth:
        place = (place + step) % depth
    return source * group + core, (place * 2 + x) * group + core


def on_device(rows_n, cols_n, left_matrix, left_pattern, right_matrix, right_pattern, keep_mask):
    group = cols_n // rows_n

    def send(value, pairs):
        pairs = [(a[0] * cols_n + a[1], b[0] * cols_n + b[1]) for a, b in pairs]
        return lax.ppermute(value, ("row", "col"), pairs)

    devices = [(r, c) for r in range(rows_n) for c in range(cols_n)]

    def moved(value, target):
        pairs = []
        for r, c in devices:
            to_r, to_c = target(r, c)
            pairs.append(((r, c), (to_r % rows_n, to_c % cols_n)))
        return send(value, pairs)

    whole, rpack = pack(left_pattern, right_pattern, left_matrix, right_matrix)
    even = moved(whole, lambda r, c: (r, c - group * (r + r % 2)))
    r0 = moved(rpack, lambda r, c: (r - c // group, c))
    r1 = moved(rpack, lambda r, c: (r - c // group - 1, c))
    roads = {at: detour(*at, cols_n, group) for at in devices}
    half = second_half(whole, rpack)
    between = send(half, [((r, roads[r, c][0]), (r, roads[r, c][1])) for r, c in devices])
    zero = blank(half, (left_matrix.shape[0], right_matrix.shape[1]))
    passed = moved(
        lax.slice_in_dim(even, 0, HALF + META),
        lambda r, c: (r, c + group * (2 * (r % 2) - 1)),
    )
    more = send(between, [((r, roads[r, c][1]), (r, c)) for r, c in devices])
    out, before, table = first(keep_mask, even, r0, r1, zero)
    return last(table, passed, more, r0, r1, before, out)


def solution(mesh):
    part = P("row", "col")
    return jax.shard_map(
        functools.partial(on_device, mesh.shape["row"], mesh.shape["col"]),
        mesh=mesh,
        in_specs=(part,) * 5,
        out_specs=part,
        check_vma=False,
    )
```

```python
import functools

import jax
import jax.numpy as jnp
from jax import lax
from jax.experimental import pallas as pl
from jax.experimental.pallas import tpu as pltpu
from jax.sharding import PartitionSpec as P

BLK = 128
MR = 32
KS = 4
NC = 8
LCAP = 16
RCAP = 4
META = 16
LROWS = LCAP * BLK
HALF = LROWS // 2
PAIRS = LCAP * RCAP
TILES = MR * NC
ZROWS = 256
ZFIRST = 6


def block_of(ref, block_row, block_col):
    return ref.at[
        pl.ds(pl.multiple_of(block_row * BLK, BLK), BLK),
        pl.ds(pl.multiple_of(block_col * BLK, BLK), BLK),
    ]


def spec(space):
    return pl.BlockSpec(memory_space=space)


def pack_left_kernel(pattern, left, out, more, pos, meta, sems):
    count = 0
    starts = []
    for k in range(KS):
        starts.append(count)
        for i in range(MR):
            pos[count] = k * MR + i
            count = count + pattern[k, i]
    starts.append(count)
    copies = []
    for a in range(LCAP):
        at = pos[a]
        block = block_of(left, at & (MR - 1), at >> 5)
        first_row = a * BLK if a * BLK < HALF else a * BLK + META
        copies.append(pltpu.make_async_copy(block, out.at[pl.ds(first_row, BLK), :], sems.at[a]))
        copies[-1].start()
        if a * BLK >= HALF:
            copies.append(
                pltpu.make_async_copy(
                    block, more.at[pl.ds(a * BLK - HALF, BLK), :], sems.at[LCAP + a - LCAP // 2]
                )
            )
            copies[-1].start()
    lane = lax.broadcasted_iota(jnp.int32, (META, BLK), 1)
    row = jnp.zeros((META, BLK), jnp.int32)
    for a in range(LCAP):
        row = jnp.where(lane == a, pos[a], row)
    for k in range(KS + 1):
        row = jnp.where(lane == LCAP + k, starts[k], row)
    meta[...] = row.astype(jnp.float32).astype(jnp.bfloat16)
    copies.append(pltpu.make_async_copy(meta, out.at[pl.ds(HALF, META), :], sems.at[LCAP + LCAP // 2]))
    copies[-1].start()
    for copy in copies:
        copy.wait()


def pack_left(pattern, left):
    return pl.pallas_call(
        pack_left_kernel,
        out_shape=(
            jax.ShapeDtypeStruct((LROWS + META, BLK), jnp.bfloat16),
            jax.ShapeDtypeStruct((HALF, BLK), jnp.bfloat16),
        ),
        in_specs=[spec(pltpu.SMEM), spec(pltpu.HBM)],
        out_specs=[spec(pl.ANY)] * 2,
        scratch_shapes=[
            pltpu.SMEM((LCAP + 1,), jnp.int32),
            pltpu.VMEM((META, BLK), jnp.bfloat16),
            pltpu.SemaphoreType.DMA((LCAP + LCAP // 2 + 1,)),
        ],
        compiler_params=pltpu.CompilerParams(vmem_limit_bytes=52 << 20),
        cost_estimate=pl.CostEstimate(flops=0, bytes_accessed=2 << 20, transcendentals=0),
        name="pack_left",
    )(pattern.T, left)


def clear(out, zero, sems, begin, end):
    zero[...] = jnp.zeros_like(zero)
    copies = [
        pltpu.make_async_copy(zero, out.at[pl.ds(n * ZROWS, ZROWS), :], sems.at[n - begin])
        for n in range(begin, end)
    ]
    for copy in copies:
        copy.start()
    return copies


def pack_right_kernel(pattern, right, after, out, product, pos, meta, sems, zero, zero_sems):
    del after
    part = lax.rem(lax.axis_index("col"), 2)
    count = 0
    for k in range(KS):
        for j in range(NC):
            pos[count] = k * NC + j
            count = count + pattern[part * KS + k, j]
    copies = []
    for b in range(RCAP):
        at = pos[b]
        copies.append(
            pltpu.make_async_copy(
                block_of(right, part * KS + (at >> 3), at & (NC - 1)),
                out.at[pl.ds(0, BLK), pl.ds(b * BLK, BLK)],
                sems.at[b],
            )
        )
        copies[-1].start()
    lane = lax.broadcasted_iota(jnp.int32, (META, RCAP * BLK), 1)
    row = jnp.zeros((META, RCAP * BLK), jnp.int32)
    for b in range(RCAP):
        row = jnp.where(lane == b, pos[b], row)
    meta[...] = row.astype(jnp.float32).astype(jnp.bfloat16)
    copies.append(pltpu.make_async_copy(meta, out.at[pl.ds(BLK, META), :], sems.at[RCAP]))
    copies[-1].start()
    copies += clear(product, zero, zero_sems, 0, ZFIRST)
    for copy in copies:
        copy.wait()


def pack_right(pattern, right, after, shape):
    return pl.pallas_call(
        pack_right_kernel,
        out_shape=(
            jax.ShapeDtypeStruct((BLK + META, RCAP * BLK), jnp.bfloat16),
            jax.ShapeDtypeStruct(shape, jnp.bfloat16),
        ),
        in_specs=[spec(pltpu.SMEM), spec(pltpu.HBM), spec(pl.ANY)],
        out_specs=[spec(pl.ANY), spec(pltpu.HBM)],
        scratch_shapes=[
            pltpu.SMEM((RCAP + 1,), jnp.int32),
            pltpu.VMEM((META, RCAP * BLK), jnp.bfloat16),
            pltpu.SemaphoreType.DMA((RCAP + 1,)),
            pltpu.VMEM((ZROWS, shape[1]), jnp.bfloat16),
            pltpu.SemaphoreType.DMA((ZFIRST,)),
        ],
        compiler_params=pltpu.CompilerParams(vmem_limit_bytes=52 << 20),
        cost_estimate=pl.CostEstimate(flops=0, bytes_accessed=1 << 20, transcendentals=0),
        name="pack_right",
    )(pattern, right, after)


def piece(code):
    return (
        pl.ds(pl.multiple_of((code >> 2) * BLK, BLK), BLK),
        pl.ds(pl.multiple_of((code & 3) * BLK, BLK), BLK),
    )


def products(halves, right, prod):
    chunk = 512
    rhs = right[...]
    for n, (ref, begin) in enumerate(halves):
        for first in range(0, HALF, chunk):
            prod[pl.ds(n * HALF + first, chunk), :] = jnp.dot(
                ref[pl.ds(begin + first, chunk), :], rhs, preferred_element_type=jnp.float32
            )


def gather(left_at, right_at, kept, owner, prod, slot_of):
    total = 0
    for b in range(RCAP):
        at = right_at(b)
        j = at & (NC - 1)

        def meet(a, total, b=b, j=j):
            target = (left_at(a) & (MR - 1)) * NC + j
            code = a * RCAP + b
            wanted = kept[target] >= 0
            held = owner[target]
            fresh = jnp.logical_and(wanted, held == 0)

            @pl.when(fresh)
            def _():
                owner[target] = code + 1
                slot_of[total] = code * TILES + target

            @pl.when(jnp.logical_and(wanted, held > 0))
            def _():
                rows, cols = piece(held - 1)
                more_rows, more_cols = piece(code)
                prod[rows, cols] += prod[more_rows, more_cols]

            return total + fresh.astype(jnp.int32)

        k = at >> 3
        total = lax.fori_loop(left_at(LCAP + k), left_at(LCAP + 1 + k), meet, total)
    return total


def write(total, value, slot_of, stage, out, sems):
    def copy_out(slot, target):
        return pltpu.make_async_copy(
            stage.at[slot], block_of(out, target >> 3, target & (NC - 1)), sems.at[slot]
        )

    def send(slot, carry):
        entry = slot_of[slot]
        target = entry & (TILES - 1)
        stage[slot] = value(entry >> 8, target).astype(jnp.bfloat16)
        copy_out(slot, target).start()
        return carry

    def drain(slot, carry):
        copy_out(slot, slot_of[slot] & (TILES - 1)).wait()
        return carry

    lax.fori_loop(0, total, send, 0)
    lax.fori_loop(0, total, drain, 0)


def choose(flag, first, second, held):
    @pl.when(flag == 0)
    def _():
        held[...] = first[pl.ds(0, BLK), :]

    @pl.when(flag != 0)
    def _():
        held[...] = second[pl.ds(0, BLK), :]


def first_kernel(
    keep, left, r0, r1, begun, out, prod, table,
    zero, zero_sems, right, stage, meta_v, meta, slot_of, meta_sem, out_sems,
):
    del begun
    odd = lax.rem(lax.axis_index("row"), 2)
    clears = clear(out, zero, zero_sems, ZFIRST, out.shape[0] // ZROWS)
    line = lax.broadcasted_iota(jnp.int32, (META, BLK), 0)
    rows = left[pl.ds(HALF, META), :].astype(jnp.float32)
    for n, ref in enumerate((r0, r1)):
        right_row = ref[pl.ds(BLK, META), pl.ds(0, BLK)].astype(jnp.float32)
        rows = jnp.where(line == 1 + n, right_row, rows)
    meta_v[...] = rows.astype(jnp.int32)
    meta_copy = pltpu.make_async_copy(meta_v, meta, meta_sem)
    meta_copy.start()
    for at in range(TILES):
        table[at] = jnp.minimum(keep[at // NC, at % NC], 1) - 1
    choose(odd, r0, r1, right)
    products(((left, 0), (left, HALF + META)), right, prod)
    meta_copy.wait()
    total = gather(
        lambda a: meta[0, a],
        lambda b: meta[1 + odd, b],
        table,
        table,
        prod,
        slot_of,
    )

    def value(code, target):
        rows, cols = piece(code)
        return prod[rows, cols]

    for copy in clears:
        copy.wait()
    write(total, value, slot_of, stage, out, out_sems)
    for b in range(RCAP):
        table[TILES + b] = meta[2 - odd, b]


def first(keep, left, r0, r1, begun):
    return pl.pallas_call(
        first_kernel,
        out_shape=(
            jax.ShapeDtypeStruct(begun.shape, begun.dtype),
            jax.ShapeDtypeStruct((LROWS, RCAP * BLK), jnp.float32),
            jax.ShapeDtypeStruct((TILES + BLK,), jnp.int32),
        ),
        in_specs=[spec(pltpu.SMEM)] + [spec(pltpu.VMEM)] * 3 + [spec(pltpu.HBM)],
        out_specs=[spec(pltpu.HBM), spec(pltpu.VMEM), spec(pltpu.SMEM)],
        scratch_shapes=[
            pltpu.VMEM((ZROWS, begun.shape[1]), jnp.bfloat16),
            pltpu.SemaphoreType.DMA((begun.shape[0] // ZROWS - ZFIRST,)),
            pltpu.VMEM((BLK, RCAP * BLK), jnp.bfloat16),
            pltpu.VMEM((PAIRS, BLK, BLK), jnp.bfloat16),
            pltpu.VMEM((META, BLK), jnp.int32),
            pltpu.SMEM((META, BLK), jnp.int32),
            pltpu.SMEM((PAIRS,), jnp.int32),
            pltpu.SemaphoreType.DMA,
            pltpu.SemaphoreType.DMA((PAIRS,)),
        ],
        input_output_aliases={4: 0},
        compiler_params=pltpu.CompilerParams(vmem_limit_bytes=32 << 20),
        cost_estimate=pl.CostEstimate(
            flops=10**10, bytes_accessed=14 << 20, transcendentals=0
        ),
        name="first",
    )(keep, left, r0, r1, begun)


def last_kernel(
    table_in, left, more, r0, r1, before, zero, out,
    table, table_sem, right, prod, stage, meta_v, meta, owner, slot_of, meta_sem, out_sems,
):
    del zero
    table_copy = pltpu.make_async_copy(table_in, table, table_sem)
    table_copy.start()
    odd = lax.rem(lax.axis_index("row"), 2)
    meta_v[...] = left[pl.ds(HALF, META), :].astype(jnp.float32).astype(jnp.int32)
    meta_copy = pltpu.make_async_copy(meta_v, meta, meta_sem)
    meta_copy.start()
    for at in range(TILES):
        owner[at] = 0
    choose(odd, r1, r0, right)
    products(((left, 0), (more, 0)), right, prod)
    meta_copy.wait()
    table_copy.wait()
    total = gather(
        lambda a: meta[0, a],
        lambda b: table[TILES + b],
        table,
        owner,
        prod,
        slot_of,
    )

    def value(code, target):
        rows, cols = piece(code)
        held = table[target]
        old_rows, old_cols = piece(jnp.maximum(held - 1, 0))
        fresh = prod[rows, cols]
        return jnp.where(held > 0, fresh + before[old_rows, old_cols], fresh)

    write(total, value, slot_of, stage, out, out_sems)


def last(table, left, more, r0, r1, before, out):
    return pl.pallas_call(
        last_kernel,
        out_shape=jax.ShapeDtypeStruct(out.shape, out.dtype),
        in_specs=[spec(pl.ANY)] + [spec(pltpu.VMEM)] * 5 + [spec(pltpu.HBM)],
        out_specs=spec(pltpu.HBM),
        scratch_shapes=[
            pltpu.SMEM(table.shape, jnp.int32),
            pltpu.SemaphoreType.DMA,
            pltpu.VMEM((BLK, RCAP * BLK), jnp.bfloat16),
            pltpu.VMEM((LROWS, RCAP * BLK), jnp.float32),
            pltpu.VMEM((PAIRS, BLK, BLK), jnp.bfloat16),
            pltpu.VMEM((META, BLK), jnp.int32),
            pltpu.SMEM((META, BLK), jnp.int32),
            pltpu.SMEM((TILES,), jnp.int32),
            pltpu.SMEM((PAIRS,), jnp.int32),
            pltpu.SemaphoreType.DMA,
            pltpu.SemaphoreType.DMA((PAIRS,)),
        ],
        input_output_aliases={6: 0},
        compiler_params=pltpu.CompilerParams(vmem_limit_bytes=32 << 20),
        cost_estimate=pl.CostEstimate(
            flops=2 * PAIRS * BLK**3, bytes_accessed=4 << 20, transcendentals=0
        ),
        name="last",
    )(table, left, more, r0, r1, before, out)


def detour(r, c, cols_n, group):
    core, chip = c % group, c // group
    z, x = chip // 2, chip % 2
    depth = cols_n // group // 2
    step = (r + r % 2) // 2 % depth
    source = (chip + r + 1 - r % 2) % (cols_n // group)
    place = source // 2
    if step == 0:
        place = z
    elif 2 * step != depth and 2 * (place - z) % (2 * depth) == depth:
        place = (place + step) % depth
    return source * group + core, (place * 2 + x) * group + core


def on_device(rows_n, cols_n, left_matrix, left_pattern, right_matrix, right_pattern, keep_mask):
    group = cols_n // rows_n

    def send(value, pairs):
        pairs = [(a[0] * cols_n + a[1], b[0] * cols_n + b[1]) for a, b in pairs]
        return lax.ppermute(value, ("row", "col"), pairs)

    devices = [(r, c) for r in range(rows_n) for c in range(cols_n)]

    def moved(value, target):
        pairs = []
        for r, c in devices:
            to_r, to_c = target(r, c)
            pairs.append(((r, c), (to_r % rows_n, to_c % cols_n)))
        return send(value, pairs)

    whole, half = pack_left(left_pattern, left_matrix)
    even = moved(whole, lambda r, c: (r, c - group * (r + r % 2)))
    roads = {at: detour(*at, cols_n, group) for at in devices}
    between = send(half, [((r, roads[r, c][0]), (r, roads[r, c][1])) for r, c in devices])
    shape = (left_matrix.shape[0], right_matrix.shape[1])
    rpack, begun = pack_right(right_pattern, right_matrix, whole, shape)
    r0 = moved(rpack, lambda r, c: (r - c // group, c))
    r1 = moved(rpack, lambda r, c: (r - c // group - 1, c))
    passed = moved(
        lax.slice_in_dim(even, 0, HALF + META),
        lambda r, c: (r, c + group * (2 * (r % 2) - 1)),
    )
    more = send(between, [((r, roads[r, c][1]), (r, c)) for r, c in devices])
    out, before, table = first(keep_mask, even, r0, r1, begun)
    return last(table, passed, more, r0, r1, before, out)


def solution(mesh):
    part = P("row", "col")
    return jax.shard_map(
        functools.partial(on_device, mesh.shape["row"], mesh.shape["col"]),
        mesh=mesh,
        in_specs=(part,) * 5,
        out_specs=part,
        check_vma=False,
    )
```

```python
import functools

import jax
import jax.numpy as jnp
from jax import lax
from jax.experimental import pallas as pl
from jax.experimental.pallas import tpu as pltpu
from jax.sharding import PartitionSpec as P

BLK = 128
MR = 32
KS = 4
NC = 8
LCAP = 16
RCAP = 4
META = 16
LROWS = LCAP * BLK
HALF = LROWS // 2
PAIRS = LCAP * RCAP
TILES = MR * NC
ZROWS = 256
NOTES = TILES + 64


def block_of(ref, block_row, block_col):
    return ref.at[
        pl.ds(pl.multiple_of(block_row * BLK, BLK), BLK),
        pl.ds(pl.multiple_of(block_col * BLK, BLK), BLK),
    ]


def spec(space):
    return pl.BlockSpec(memory_space=space)


def pack_left_kernel(pattern, left, out, more, pos, meta, sems):
    count = 0
    starts = []
    for k in range(KS):
        starts.append(count)
        for i in range(MR):
            pos[count] = k * MR + i
            count = count + pattern[k, i]
    starts.append(count)
    copies = []
    for a in range(LCAP):
        at = pos[a]
        block = block_of(left, at & (MR - 1), at >> 5)
        first_row = a * BLK if a * BLK < HALF else a * BLK + META
        copies.append(pltpu.make_async_copy(block, out.at[pl.ds(first_row, BLK), :], sems.at[a]))
        copies[-1].start()
        if a * BLK >= HALF:
            copies.append(
                pltpu.make_async_copy(
                    block, more.at[pl.ds(a * BLK - HALF, BLK), :], sems.at[LCAP + a - LCAP // 2]
                )
            )
            copies[-1].start()
    lane = lax.broadcasted_iota(jnp.int32, (META, BLK), 1)
    row = jnp.zeros((META, BLK), jnp.int32)
    for a in range(LCAP):
        row = jnp.where(lane == a, pos[a], row)
    for k in range(KS + 1):
        row = jnp.where(lane == LCAP + k, starts[k], row)
    meta[...] = row.astype(jnp.float32).astype(jnp.bfloat16)
    copies.append(pltpu.make_async_copy(meta, out.at[pl.ds(HALF, META), :], sems.at[LCAP + LCAP // 2]))
    copies[-1].start()
    for copy in copies:
        copy.wait()


def pack_left(pattern, left):
    return pl.pallas_call(
        pack_left_kernel,
        out_shape=(
            jax.ShapeDtypeStruct((LROWS + META, BLK), jnp.bfloat16),
            jax.ShapeDtypeStruct((HALF, BLK), jnp.bfloat16),
        ),
        in_specs=[spec(pltpu.SMEM), spec(pltpu.HBM)],
        out_specs=[spec(pl.ANY)] * 2,
        scratch_shapes=[
            pltpu.SMEM((LCAP + 1,), jnp.int32),
            pltpu.VMEM((META, BLK), jnp.bfloat16),
            pltpu.SemaphoreType.DMA((LCAP + LCAP // 2 + 1,)),
        ],
        compiler_params=pltpu.CompilerParams(vmem_limit_bytes=52 << 20),
        cost_estimate=pl.CostEstimate(flops=0, bytes_accessed=2 << 20, transcendentals=0),
        name="pack_left",
    )(pattern.T, left)


def pack_right_kernel(pattern, right, after, out, pos, meta, sems):
    del after
    part = lax.rem(lax.axis_index("col"), 2)
    count = 0
    for k in range(KS):
        for j in range(NC):
            pos[count] = k * NC + j
            count = count + pattern[part * KS + k, j]
    copies = []
    for b in range(RCAP):
        at = pos[b]
        copies.append(
            pltpu.make_async_copy(
                block_of(right, part * KS + (at >> 3), at & (NC - 1)),
                out.at[pl.ds(0, BLK), pl.ds(b * BLK, BLK)],
                sems.at[b],
            )
        )
        copies[-1].start()
    lane = lax.broadcasted_iota(jnp.int32, (META, RCAP * BLK), 1)
    row = jnp.zeros((META, RCAP * BLK), jnp.int32)
    for b in range(RCAP):
        row = jnp.where(lane == b, pos[b], row)
    meta[...] = row.astype(jnp.float32).astype(jnp.bfloat16)
    copies.append(pltpu.make_async_copy(meta, out.at[pl.ds(BLK, META), :], sems.at[RCAP]))
    copies[-1].start()
    for copy in copies:
        copy.wait()


def pack_right(pattern, right, after):
    return pl.pallas_call(
        pack_right_kernel,
        out_shape=jax.ShapeDtypeStruct((BLK + META, RCAP * BLK), jnp.bfloat16),
        in_specs=[spec(pltpu.SMEM), spec(pltpu.HBM), spec(pl.ANY)],
        out_specs=spec(pl.ANY),
        scratch_shapes=[
            pltpu.SMEM((RCAP + 1,), jnp.int32),
            pltpu.VMEM((META, RCAP * BLK), jnp.bfloat16),
            pltpu.SemaphoreType.DMA((RCAP + 1,)),
        ],
        compiler_params=pltpu.CompilerParams(vmem_limit_bytes=52 << 20),
        cost_estimate=pl.CostEstimate(flops=0, bytes_accessed=1 << 20, transcendentals=0),
        name="pack_right",
    )(pattern, right, after)


def piece(code):
    return (
        pl.ds(pl.multiple_of((code >> 2) * BLK, BLK), BLK),
        pl.ds(pl.multiple_of((code & 3) * BLK, BLK), BLK),
    )


def products(halves, right, prod):
    chunk = 512
    rhs = right[...]
    for n, (ref, begin) in enumerate(halves):
        for first in range(0, HALF, chunk):
            prod[pl.ds(n * HALF + first, chunk), :] = jnp.dot(
                ref[pl.ds(begin + first, chunk), :], rhs, preferred_element_type=jnp.float32
            )


def gather(left_at, right_at, kept, owner, prod, slot_of):
    total = 0
    for b in range(RCAP):
        at = right_at(b)
        j = at & (NC - 1)

        def meet(a, total, b=b, j=j):
            target = (left_at(a) & (MR - 1)) * NC + j
            code = a * RCAP + b
            wanted = kept[target] >= 0
            held = owner[target]
            fresh = jnp.logical_and(wanted, held == 0)

            @pl.when(fresh)
            def _():
                owner[target] = code + 1
                slot_of[total] = code * TILES + target

            @pl.when(jnp.logical_and(wanted, held > 0))
            def _():
                rows, cols = piece(held - 1)
                more_rows, more_cols = piece(code)
                prod[rows, cols] += prod[more_rows, more_cols]

            return total + fresh.astype(jnp.int32)

        k = at >> 3
        total = lax.fori_loop(left_at(LCAP + k), left_at(LCAP + 1 + k), meet, total)
    return total


def choose(flag, first, second, held):
    @pl.when(flag == 0)
    def _():
        held[...] = first[pl.ds(0, BLK), :]

    @pl.when(flag != 0)
    def _():
        held[...] = second[pl.ds(0, BLK), :]


def first_kernel(
    keep, left, r0, r1, out, prod, table,
    zero, zero_sems, right, meta_v, meta, slot_of, meta_sem,
):
    zero[...] = jnp.zeros_like(zero)
    clears = [
        pltpu.make_async_copy(zero, out.at[pl.ds(n * ZROWS, ZROWS), :], zero_sems.at[n])
        for n in range(out.shape[0] // ZROWS)
    ]
    for copy in clears:
        copy.start()
    odd = lax.rem(lax.axis_index("row"), 2)
    line = lax.broadcasted_iota(jnp.int32, (META, BLK), 0)
    rows = left[pl.ds(HALF, META), :].astype(jnp.float32)
    for n, ref in enumerate((r0, r1)):
        right_row = ref[pl.ds(BLK, META), pl.ds(0, BLK)].astype(jnp.float32)
        rows = jnp.where(line == 1 + n, right_row, rows)
    meta_v[...] = rows.astype(jnp.int32)
    meta_copy = pltpu.make_async_copy(meta_v, meta, meta_sem)
    meta_copy.start()
    for at in range(TILES):
        table[at] = jnp.minimum(keep[at // NC, at % NC], 1) - 1
    choose(odd, r0, r1, right)
    products(((left, 0), (left, HALF + META)), right, prod)
    meta_copy.wait()
    total = gather(
        lambda a: meta[0, a],
        lambda b: meta[1 + odd, b],
        table,
        table,
        prod,
        slot_of,
    )

    for b in range(RCAP):
        table[TILES + b] = meta[2 - odd, b]
    table[TILES + RCAP] = total

    def note(slot, carry):
        table[NOTES + slot] = slot_of[slot]
        return carry

    lax.fori_loop(0, total, note, 0)
    for copy in clears:
        copy.wait()


def first(keep, left, r0, r1):
    return pl.pallas_call(
        first_kernel,
        out_shape=(
            jax.ShapeDtypeStruct((MR * BLK, NC * BLK), jnp.bfloat16),
            jax.ShapeDtypeStruct((LROWS, RCAP * BLK), jnp.float32),
            jax.ShapeDtypeStruct((NOTES + PAIRS,), jnp.int32),
        ),
        in_specs=[spec(pltpu.SMEM)] + [spec(pltpu.VMEM)] * 3,
        out_specs=[spec(pltpu.HBM), spec(pltpu.VMEM), spec(pltpu.SMEM)],
        scratch_shapes=[
            pltpu.VMEM((ZROWS, NC * BLK), jnp.bfloat16),
            pltpu.SemaphoreType.DMA((MR * BLK // ZROWS,)),
            pltpu.VMEM((BLK, RCAP * BLK), jnp.bfloat16),
            pltpu.VMEM((META, BLK), jnp.int32),
            pltpu.SMEM((META, BLK), jnp.int32),
            pltpu.SMEM((PAIRS,), jnp.int32),
            pltpu.SemaphoreType.DMA,
        ],
        compiler_params=pltpu.CompilerParams(vmem_limit_bytes=32 << 20),
        cost_estimate=pl.CostEstimate(
            flops=10**10, bytes_accessed=14 << 20, transcendentals=0
        ),
        name="first",
    )(keep, left, r0, r1)


def last_kernel(
    table_in, left, more, r0, r1, before, zero, out,
    table, table_sem, right, prod, stage, meta_v, meta, owner, slot_of, meta_sem, out_sems,
):
    del zero
    table_copy = pltpu.make_async_copy(table_in, table, table_sem)
    table_copy.start()
    odd = lax.rem(lax.axis_index("row"), 2)
    meta_v[...] = left[pl.ds(HALF, META), :].astype(jnp.float32).astype(jnp.int32)
    meta_copy = pltpu.make_async_copy(meta_v, meta, meta_sem)
    meta_copy.start()
    for at in range(TILES):
        owner[at] = 0
    choose(odd, r1, r0, right)
    products(((left, 0), (more, 0)), right, prod)
    meta_copy.wait()
    table_copy.wait()
    total = gather(
        lambda a: meta[0, a],
        lambda b: table[TILES + b],
        table,
        owner,
        prod,
        slot_of,
    )

    def copy_out(slot, target):
        return pltpu.make_async_copy(
            stage.at[slot], block_of(out, target >> 3, target & (NC - 1)), out_sems.at[slot]
        )

    def send(slot, carry):
        entry = slot_of[slot]
        target = entry & (TILES - 1)
        rows, cols = piece(entry >> 8)
        fresh = prod[rows, cols]
        held = table[target]
        old_rows, old_cols = piece(jnp.maximum(held - 1, 0))
        both = jnp.where(held > 0, fresh + before[old_rows, old_cols], fresh)
        stage[slot] = both.astype(jnp.bfloat16)
        copy_out(slot, target).start()
        return carry

    def send_old(n, slot):
        entry = table[NOTES + n]
        target = entry & (TILES - 1)
        alone = owner[target] == 0

        @pl.when(alone)
        def _():
            rows, cols = piece(entry >> 8)
            slot_of[slot] = entry
            stage[slot] = before[rows, cols].astype(jnp.bfloat16)
            copy_out(slot, target).start()

        return slot + alone.astype(jnp.int32)

    def drain(slot, carry):
        copy_out(slot, slot_of[slot] & (TILES - 1)).wait()
        return carry

    lax.fori_loop(0, total, send, 0)
    slots = lax.fori_loop(0, table[TILES + RCAP], send_old, total)
    lax.fori_loop(0, slots, drain, 0)


def last(table, left, more, r0, r1, before, out):
    return pl.pallas_call(
        last_kernel,
        out_shape=jax.ShapeDtypeStruct(out.shape, out.dtype),
        in_specs=[spec(pl.ANY)] + [spec(pltpu.VMEM)] * 5 + [spec(pltpu.HBM)],
        out_specs=spec(pltpu.HBM),
        scratch_shapes=[
            pltpu.SMEM(table.shape, jnp.int32),
            pltpu.SemaphoreType.DMA,
            pltpu.VMEM((BLK, RCAP * BLK), jnp.bfloat16),
            pltpu.VMEM((LROWS, RCAP * BLK), jnp.float32),
            pltpu.VMEM((2 * PAIRS, BLK, BLK), jnp.bfloat16),
            pltpu.VMEM((META, BLK), jnp.int32),
            pltpu.SMEM((META, BLK), jnp.int32),
            pltpu.SMEM((TILES,), jnp.int32),
            pltpu.SMEM((2 * PAIRS,), jnp.int32),
            pltpu.SemaphoreType.DMA,
            pltpu.SemaphoreType.DMA((2 * PAIRS,)),
        ],
        input_output_aliases={6: 0},
        compiler_params=pltpu.CompilerParams(vmem_limit_bytes=32 << 20),
        cost_estimate=pl.CostEstimate(
            flops=2 * PAIRS * BLK**3, bytes_accessed=4 << 20, transcendentals=0
        ),
        name="last",
    )(table, left, more, r0, r1, before, out)


def detour(r, c, cols_n, group):
    core, chip = c % group, c // group
    z, x = chip // 2, chip % 2
    depth = cols_n // group // 2
    step = (r + r % 2) // 2 % depth
    source = (chip + r + 1 - r % 2) % (cols_n // group)
    place = source // 2
    if step == 0:
        place = z
    elif 2 * step != depth and 2 * (place - z) % (2 * depth) == depth:
        place = (place + step) % depth
    return source * group + core, (place * 2 + x) * group + core


def on_device(rows_n, cols_n, left_matrix, left_pattern, right_matrix, right_pattern, keep_mask):
    group = cols_n // rows_n

    def send(value, pairs):
        pairs = [(a[0] * cols_n + a[1], b[0] * cols_n + b[1]) for a, b in pairs]
        return lax.ppermute(value, ("row", "col"), pairs)

    devices = [(r, c) for r in range(rows_n) for c in range(cols_n)]

    def moved(value, target):
        pairs = []
        for r, c in devices:
            to_r, to_c = target(r, c)
            pairs.append(((r, c), (to_r % rows_n, to_c % cols_n)))
        return send(value, pairs)

    whole, half = pack_left(left_pattern, left_matrix)
    even = moved(whole, lambda r, c: (r, c - group * (r + r % 2)))
    roads = {at: detour(*at, cols_n, group) for at in devices}
    between = send(half, [((r, roads[r, c][0]), (r, roads[r, c][1])) for r, c in devices])
    rpack = pack_right(right_pattern, right_matrix, whole)
    r0 = moved(rpack, lambda r, c: (r - c // group, c))
    r1 = moved(rpack, lambda r, c: (r - c // group - 1, c))
    passed = moved(
        lax.slice_in_dim(even, 0, HALF + META),
        lambda r, c: (r, c + group * (2 * (r % 2) - 1)),
    )
    more = send(between, [((r, roads[r, c][1]), (r, c)) for r, c in devices])
    out, before, table = first(keep_mask, even, r0, r1)
    return last(table, passed, more, r0, r1, before, out)


def solution(mesh):
    part = P("row", "col")
    return jax.shard_map(
        functools.partial(on_device, mesh.shape["row"], mesh.shape["col"]),
        mesh=mesh,
        in_specs=(part,) * 5,
        out_specs=part,
        check_vma=False,
    )
```

```python
import functools

import jax
import jax.numpy as jnp
from jax import lax
from jax.experimental import pallas as pl
from jax.experimental.pallas import tpu as pltpu
from jax.sharding import PartitionSpec as P

BLK = 128
MR = 32
KS = 4
NC = 8
LCAP = 16
RCAP = 4
META = 16
LROWS = LCAP * BLK
HALF = LROWS // 2
PAIRS = LCAP * RCAP
TILES = MR * NC
ZROWS = 256


def block_of(ref, block_row, block_col):
    return ref.at[
        pl.ds(pl.multiple_of(block_row * BLK, BLK), BLK),
        pl.ds(pl.multiple_of(block_col * BLK, BLK), BLK),
    ]


def spec(space):
    return pl.BlockSpec(memory_space=space)


def pack_left_kernel(pattern, left, out, more, pos, meta, sems):
    count = 0
    starts = []
    for k in range(KS):
        starts.append(count)
        for i in range(MR):
            pos[count] = k * MR + i
            count = count + pattern[k, i]
    starts.append(count)
    copies = []
    for a in range(LCAP):
        at = pos[a]
        block = block_of(left, at & (MR - 1), at >> 5)
        first_row = a * BLK if a * BLK < HALF else a * BLK + META
        copies.append(pltpu.make_async_copy(block, out.at[pl.ds(first_row, BLK), :], sems.at[a]))
        copies[-1].start()
        if a * BLK >= HALF:
            copies.append(
                pltpu.make_async_copy(
                    block, more.at[pl.ds(a * BLK - HALF, BLK), :], sems.at[LCAP + a - LCAP // 2]
                )
            )
            copies[-1].start()
    lane = lax.broadcasted_iota(jnp.int32, (META, BLK), 1)
    row = jnp.zeros((META, BLK), jnp.int32)
    for a in range(LCAP):
        row = jnp.where(lane == a, pos[a], row)
    for k in range(KS + 1):
        row = jnp.where(lane == LCAP + k, starts[k], row)
    meta[...] = row.astype(jnp.float32).astype(jnp.bfloat16)
    copies.append(pltpu.make_async_copy(meta, out.at[pl.ds(HALF, META), :], sems.at[LCAP + LCAP // 2]))
    copies[-1].start()
    for copy in copies:
        copy.wait()


def pack_left(pattern, left):
    return pl.pallas_call(
        pack_left_kernel,
        out_shape=(
            jax.ShapeDtypeStruct((LROWS + META, BLK), jnp.bfloat16),
            jax.ShapeDtypeStruct((HALF, BLK), jnp.bfloat16),
        ),
        in_specs=[spec(pltpu.SMEM), spec(pltpu.HBM)],
        out_specs=[spec(pl.ANY)] * 2,
        scratch_shapes=[
            pltpu.SMEM((LCAP + 1,), jnp.int32),
            pltpu.VMEM((META, BLK), jnp.bfloat16),
            pltpu.SemaphoreType.DMA((LCAP + LCAP // 2 + 1,)),
        ],
        compiler_params=pltpu.CompilerParams(vmem_limit_bytes=52 << 20),
        cost_estimate=pl.CostEstimate(flops=0, bytes_accessed=2 << 20, transcendentals=0),
        name="pack_left",
    )(pattern.T, left)


def pack_right_kernel(pattern, right, after, out, pos, meta, sems):
    del after
    part = lax.rem(lax.axis_index("col"), 2)
    count = 0
    for k in range(KS):
        for j in range(NC):
            pos[count] = k * NC + j
            count = count + pattern[part * KS + k, j]
    copies = []
    for b in range(RCAP):
        at = pos[b]
        copies.append(
            pltpu.make_async_copy(
                block_of(right, part * KS + (at >> 3), at & (NC - 1)),
                out.at[pl.ds(0, BLK), pl.ds(b * BLK, BLK)],
                sems.at[b],
            )
        )
        copies[-1].start()
    lane = lax.broadcasted_iota(jnp.int32, (META, RCAP * BLK), 1)
    row = jnp.zeros((META, RCAP * BLK), jnp.int32)
    for b in range(RCAP):
        row = jnp.where(lane == b, pos[b], row)
    meta[...] = row.astype(jnp.float32).astype(jnp.bfloat16)
    copies.append(pltpu.make_async_copy(meta, out.at[pl.ds(BLK, META), :], sems.at[RCAP]))
    copies[-1].start()
    for copy in copies:
        copy.wait()


def pack_right(pattern, right, after):
    return pl.pallas_call(
        pack_right_kernel,
        out_shape=jax.ShapeDtypeStruct((BLK + META, RCAP * BLK), jnp.bfloat16),
        in_specs=[spec(pltpu.SMEM), spec(pltpu.HBM), spec(pl.ANY)],
        out_specs=spec(pl.ANY),
        scratch_shapes=[
            pltpu.SMEM((RCAP + 1,), jnp.int32),
            pltpu.VMEM((META, RCAP * BLK), jnp.bfloat16),
            pltpu.SemaphoreType.DMA((RCAP + 1,)),
        ],
        compiler_params=pltpu.CompilerParams(vmem_limit_bytes=52 << 20),
        cost_estimate=pl.CostEstimate(flops=0, bytes_accessed=1 << 20, transcendentals=0),
        name="pack_right",
    )(pattern, right, after)


def piece(code):
    return (
        pl.ds(pl.multiple_of((code >> 2) * BLK, BLK), BLK),
        pl.ds(pl.multiple_of((code & 3) * BLK, BLK), BLK),
    )


def products(halves, right, prod):
    chunk = 512
    rhs = right[...]
    for n, (ref, begin) in enumerate(halves):
        for first in range(0, HALF, chunk):
            prod[pl.ds(n * HALF + first, chunk), :] = jnp.dot(
                ref[pl.ds(begin + first, chunk), :], rhs, preferred_element_type=jnp.float32
            )


def gather(left_at, right_at, kept, owner, prod, slot_of):
    total = 0
    for b in range(RCAP):
        at = right_at(b)
        j = at & (NC - 1)

        def meet(a, total, b=b, j=j):
            target = (left_at(a) & (MR - 1)) * NC + j
            code = a * RCAP + b
            wanted = kept[target] >= 0
            held = owner[target]
            fresh = jnp.logical_and(wanted, held == 0)

            @pl.when(fresh)
            def _():
                owner[target] = code + 1
                slot_of[total] = code * TILES + target

            @pl.when(jnp.logical_and(wanted, held > 0))
            def _():
                rows, cols = piece(held - 1)
                more_rows, more_cols = piece(code)
                prod[rows, cols] += prod[more_rows, more_cols]

            return total + fresh.astype(jnp.int32)

        k = at >> 3
        total = lax.fori_loop(left_at(LCAP + k), left_at(LCAP + 1 + k), meet, total)
    return total


def write(total, value, slot_of, stage, out, sems):
    def copy_out(slot, target):
        return pltpu.make_async_copy(
            stage.at[slot], block_of(out, target >> 3, target & (NC - 1)), sems.at[slot]
        )

    def send(slot, carry):
        entry = slot_of[slot]
        target = entry & (TILES - 1)
        stage[slot] = value(entry >> 8, target).astype(jnp.bfloat16)
        copy_out(slot, target).start()
        return carry

    def drain(slot, carry):
        copy_out(slot, slot_of[slot] & (TILES - 1)).wait()
        return carry

    lax.fori_loop(0, total, send, 0)
    lax.fori_loop(0, total, drain, 0)


def choose(flag, first, second, held):
    @pl.when(flag == 0)
    def _():
        held[...] = first[pl.ds(0, BLK), :]

    @pl.when(flag != 0)
    def _():
        held[...] = second[pl.ds(0, BLK), :]


def first_kernel(
    keep, left, r0, r1, out, prod, table,
    zero, zero_sems, right, stage, meta_v, meta, slot_of, meta_sem, out_sems,
):
    odd = lax.rem(lax.axis_index("row"), 2)
    line = lax.broadcasted_iota(jnp.int32, (META, BLK), 0)
    rows = left[pl.ds(HALF, META), :].astype(jnp.float32)
    for n, ref in enumerate((r0, r1)):
        right_row = ref[pl.ds(BLK, META), pl.ds(0, BLK)].astype(jnp.float32)
        rows = jnp.where(line == 1 + n, right_row, rows)
    meta_v[...] = rows.astype(jnp.int32)
    meta_copy = pltpu.make_async_copy(meta_v, meta, meta_sem)
    meta_copy.start()
    zero[...] = jnp.zeros_like(zero)
    clears = [
        pltpu.make_async_copy(zero, out.at[pl.ds(n * ZROWS, ZROWS), :], zero_sems.at[n])
        for n in range(out.shape[0] // ZROWS)
    ]
    for copy in clears:
        copy.start()
    for at in range(TILES):
        table[at] = jnp.minimum(keep[at // NC, at % NC], 1) - 1
    choose(odd, r0, r1, right)
    products(((left, 0), (left, HALF + META)), right, prod)
    meta_copy.wait()
    total = gather(
        lambda a: meta[0, a],
        lambda b: meta[1 + odd, b],
        table,
        table,
        prod,
        slot_of,
    )

    for b in range(RCAP):
        table[TILES + b] = meta[2 - odd, b]
    for copy in clears:
        copy.wait()

    def value(code, target):
        rows, cols = piece(code)
        return prod[rows, cols]

    write(total, value, slot_of, stage, out, out_sems)


def first(keep, left, r0, r1):
    return pl.pallas_call(
        first_kernel,
        out_shape=(
            jax.ShapeDtypeStruct((MR * BLK, NC * BLK), jnp.bfloat16),
            jax.ShapeDtypeStruct((LROWS, RCAP * BLK), jnp.float32),
            jax.ShapeDtypeStruct((TILES + BLK,), jnp.int32),
        ),
        in_specs=[spec(pltpu.SMEM)] + [spec(pltpu.VMEM)] * 3,
        out_specs=[spec(pltpu.HBM), spec(pltpu.VMEM), spec(pltpu.SMEM)],
        scratch_shapes=[
            pltpu.VMEM((ZROWS, NC * BLK), jnp.bfloat16),
            pltpu.SemaphoreType.DMA((MR * BLK // ZROWS,)),
            pltpu.VMEM((BLK, RCAP * BLK), jnp.bfloat16),
            pltpu.VMEM((PAIRS, BLK, BLK), jnp.bfloat16),
            pltpu.VMEM((META, BLK), jnp.int32),
            pltpu.SMEM((META, BLK), jnp.int32),
            pltpu.SMEM((PAIRS,), jnp.int32),
            pltpu.SemaphoreType.DMA,
            pltpu.SemaphoreType.DMA((PAIRS,)),
        ],
        compiler_params=pltpu.CompilerParams(vmem_limit_bytes=32 << 20),
        cost_estimate=pl.CostEstimate(
            flops=10**10, bytes_accessed=14 << 20, transcendentals=0
        ),
        name="first",
    )(keep, left, r0, r1)


def last_kernel(
    table_in, left, more, r0, r1, before, zero, out,
    table, table_sem, right, prod, stage, meta_v, meta, owner, slot_of, meta_sem, out_sems,
):
    del zero
    table_copy = pltpu.make_async_copy(table_in, table, table_sem)
    table_copy.start()
    odd = lax.rem(lax.axis_index("row"), 2)
    meta_v[...] = left[pl.ds(HALF, META), :].astype(jnp.float32).astype(jnp.int32)
    meta_copy = pltpu.make_async_copy(meta_v, meta, meta_sem)
    meta_copy.start()
    for at in range(TILES):
        owner[at] = 0
    choose(odd, r1, r0, right)
    products(((left, 0), (more, 0)), right, prod)
    meta_copy.wait()
    table_copy.wait()
    total = gather(
        lambda a: meta[0, a],
        lambda b: table[TILES + b],
        table,
        owner,
        prod,
        slot_of,
    )

    def value(code, target):
        rows, cols = piece(code)
        fresh = prod[rows, cols]
        held = table[target]
        old_rows, old_cols = piece(jnp.maximum(held - 1, 0))
        return jnp.where(held > 0, fresh + before[old_rows, old_cols], fresh)

    write(total, value, slot_of, stage, out, out_sems)


def last(table, left, more, r0, r1, before, out):
    return pl.pallas_call(
        last_kernel,
        out_shape=jax.ShapeDtypeStruct(out.shape, out.dtype),
        in_specs=[spec(pl.ANY)] + [spec(pltpu.VMEM)] * 5 + [spec(pltpu.HBM)],
        out_specs=spec(pltpu.HBM),
        scratch_shapes=[
            pltpu.SMEM(table.shape, jnp.int32),
            pltpu.SemaphoreType.DMA,
            pltpu.VMEM((BLK, RCAP * BLK), jnp.bfloat16),
            pltpu.VMEM((LROWS, RCAP * BLK), jnp.float32),
            pltpu.VMEM((PAIRS, BLK, BLK), jnp.bfloat16),
            pltpu.VMEM((META, BLK), jnp.int32),
            pltpu.SMEM((META, BLK), jnp.int32),
            pltpu.SMEM((TILES,), jnp.int32),
            pltpu.SMEM((PAIRS,), jnp.int32),
            pltpu.SemaphoreType.DMA,
            pltpu.SemaphoreType.DMA((PAIRS,)),
        ],
        input_output_aliases={6: 0},
        compiler_params=pltpu.CompilerParams(vmem_limit_bytes=32 << 20),
        cost_estimate=pl.CostEstimate(
            flops=2 * PAIRS * BLK**3, bytes_accessed=4 << 20, transcendentals=0
        ),
        name="last",
    )(table, left, more, r0, r1, before, out)


def detour(r, c, cols_n, group):
    core, chip = c % group, c // group
    z, x = chip // 2, chip % 2
    depth = cols_n // group // 2
    step = (r + r % 2) // 2 % depth
    source = (chip + r + 1 - r % 2) % (cols_n // group)
    place = source // 2
    if step == 0:
        place = z
    elif 2 * step != depth and 2 * (place - z) % (2 * depth) == depth:
        place = (place + step) % depth
    return source * group + core, (place * 2 + x) * group + core


def on_device(rows_n, cols_n, left_matrix, left_pattern, right_matrix, right_pattern, keep_mask):
    group = cols_n // rows_n

    def send(value, pairs):
        pairs = [(a[0] * cols_n + a[1], b[0] * cols_n + b[1]) for a, b in pairs]
        return lax.ppermute(value, ("row", "col"), pairs)

    devices = [(r, c) for r in range(rows_n) for c in range(cols_n)]

    def moved(value, target):
        pairs = []
        for r, c in devices:
            to_r, to_c = target(r, c)
            pairs.append(((r, c), (to_r % rows_n, to_c % cols_n)))
        return send(value, pairs)

    whole, half = pack_left(left_pattern, left_matrix)
    even = moved(whole, lambda r, c: (r, c - group * (r + r % 2)))
    roads = {at: detour(*at, cols_n, group) for at in devices}
    between = send(half, [((r, roads[r, c][0]), (r, roads[r, c][1])) for r, c in devices])
    rpack = pack_right(right_pattern, right_matrix, whole)
    r0 = moved(rpack, lambda r, c: (r - c // group, c))
    r1 = moved(rpack, lambda r, c: (r - c // group - 1, c))
    passed = moved(
        lax.slice_in_dim(even, 0, HALF + META),
        lambda r, c: (r, c + group * (2 * (r % 2) - 1)),
    )
    more = send(between, [((r, roads[r, c][1]), (r, c)) for r, c in devices])
    out, before, table = first(keep_mask, even, r0, r1)
    return last(table, passed, more, r0, r1, before, out)


def solution(mesh):
    part = P("row", "col")
    return jax.shard_map(
        functools.partial(on_device, mesh.shape["row"], mesh.shape["col"]),
        mesh=mesh,
        in_specs=(part,) * 5,
        out_specs=part,
        check_vma=False,
    )
```

```python
import functools

import jax
import jax.numpy as jnp
from jax import lax
from jax.experimental import pallas as pl
from jax.experimental.pallas import tpu as pltpu
from jax.sharding import PartitionSpec as P

BLK = 128
MR = 32
KS = 4
NC = 8
LCAP = 16
RCAP = 4
META = 16
LROWS = LCAP * BLK
HALF = LROWS // 2
PAIRS = LCAP * RCAP
TILES = MR * NC


def block_of(ref, block_row, block_col):
    return ref.at[
        pl.ds(pl.multiple_of(block_row * BLK, BLK), BLK),
        pl.ds(pl.multiple_of(block_col * BLK, BLK), BLK),
    ]


def spec(space):
    return pl.BlockSpec(memory_space=space)


def pack_left_kernel(pattern, left, out, more, pos, meta, sems):
    count = 0
    starts = []
    for k in range(KS):
        starts.append(count)
        for i in range(MR):
            pos[count] = k * MR + i
            count = count + pattern[k, i]
    starts.append(count)
    copies = []
    for a in range(LCAP):
        at = pos[a]
        block = block_of(left, at & (MR - 1), at >> 5)
        first_row = a * BLK if a * BLK < HALF else a * BLK + META
        copies.append(pltpu.make_async_copy(block, out.at[pl.ds(first_row, BLK), :], sems.at[a]))
        copies[-1].start()
        if a * BLK >= HALF:
            copies.append(
                pltpu.make_async_copy(
                    block, more.at[pl.ds(a * BLK - HALF, BLK), :], sems.at[LCAP + a - LCAP // 2]
                )
            )
            copies[-1].start()
    lane = lax.broadcasted_iota(jnp.int32, (META, BLK), 1)
    row = jnp.zeros((META, BLK), jnp.int32)
    for a in range(LCAP):
        row = jnp.where(lane == a, pos[a], row)
    for k in range(KS + 1):
        row = jnp.where(lane == LCAP + k, starts[k], row)
    meta[...] = row.astype(jnp.float32).astype(jnp.bfloat16)
    copies.append(pltpu.make_async_copy(meta, out.at[pl.ds(HALF, META), :], sems.at[LCAP + LCAP // 2]))
    copies[-1].start()
    for copy in copies:
        copy.wait()


def pack_left(pattern, left):
    return pl.pallas_call(
        pack_left_kernel,
        out_shape=(
            jax.ShapeDtypeStruct((LROWS + META, BLK), jnp.bfloat16),
            jax.ShapeDtypeStruct((HALF, BLK), jnp.bfloat16),
        ),
        in_specs=[spec(pltpu.SMEM), spec(pltpu.HBM)],
        out_specs=[spec(pl.ANY)] * 2,
        scratch_shapes=[
            pltpu.SMEM((LCAP + 1,), jnp.int32),
            pltpu.VMEM((META, BLK), jnp.bfloat16),
            pltpu.SemaphoreType.DMA((LCAP + LCAP // 2 + 1,)),
        ],
        compiler_params=pltpu.CompilerParams(vmem_limit_bytes=52 << 20),
        cost_estimate=pl.CostEstimate(flops=0, bytes_accessed=2 << 20, transcendentals=0),
        name="pack_left",
    )(pattern.T, left)


def pack_right_kernel(pattern, right, after, out, pos, meta, sems):
    del after
    part = lax.rem(lax.axis_index("col"), 2)
    count = 0
    for k in range(KS):
        for j in range(NC):
            pos[count] = k * NC + j
            count = count + pattern[part * KS + k, j]
    copies = []
    for b in range(RCAP):
        at = pos[b]
        copies.append(
            pltpu.make_async_copy(
                block_of(right, part * KS + (at >> 3), at & (NC - 1)),
                out.at[pl.ds(0, BLK), pl.ds(b * BLK, BLK)],
                sems.at[b],
            )
        )
        copies[-1].start()
    lane = lax.broadcasted_iota(jnp.int32, (META, RCAP * BLK), 1)
    row = jnp.zeros((META, RCAP * BLK), jnp.int32)
    for b in range(RCAP):
        row = jnp.where(lane == b, pos[b], row)
    meta[...] = row.astype(jnp.float32).astype(jnp.bfloat16)
    copies.append(pltpu.make_async_copy(meta, out.at[pl.ds(BLK, META), :], sems.at[RCAP]))
    copies[-1].start()
    for copy in copies:
        copy.wait()


def pack_right(pattern, right, after):
    return pl.pallas_call(
        pack_right_kernel,
        out_shape=jax.ShapeDtypeStruct((BLK + META, RCAP * BLK), jnp.bfloat16),
        in_specs=[spec(pltpu.SMEM), spec(pltpu.HBM), spec(pl.ANY)],
        out_specs=spec(pl.ANY),
        scratch_shapes=[
            pltpu.SMEM((RCAP + 1,), jnp.int32),
            pltpu.VMEM((META, RCAP * BLK), jnp.bfloat16),
            pltpu.SemaphoreType.DMA((RCAP + 1,)),
        ],
        compiler_params=pltpu.CompilerParams(vmem_limit_bytes=52 << 20),
        cost_estimate=pl.CostEstimate(flops=0, bytes_accessed=1 << 20, transcendentals=0),
        name="pack_right",
    )(pattern, right, after)


def blank_kernel(after, out, zero, sems):
    del after
    zero[...] = jnp.zeros_like(zero)
    rows = zero.shape[0]
    copies = [
        pltpu.make_async_copy(zero, out.at[pl.ds(n * rows, rows), :], sems.at[n])
        for n in range(out.shape[0] // rows)
    ]
    for copy in copies:
        copy.start()
    for copy in copies:
        copy.wait()


def blank(after, shape):
    rows = 256
    return pl.pallas_call(
        blank_kernel,
        out_shape=jax.ShapeDtypeStruct(shape, jnp.bfloat16),
        in_specs=[spec(pl.ANY)],
        out_specs=spec(pltpu.HBM),
        scratch_shapes=[
            pltpu.VMEM((rows, shape[1]), jnp.bfloat16),
            pltpu.SemaphoreType.DMA((shape[0] // rows,)),
        ],
        cost_estimate=pl.CostEstimate(
            flops=0, bytes_accessed=2 * shape[0] * shape[1], transcendentals=0
        ),
        name="blank",
    )(after)


def piece(code):
    return (
        pl.ds(pl.multiple_of((code >> 2) * BLK, BLK), BLK),
        pl.ds(pl.multiple_of((code & 3) * BLK, BLK), BLK),
    )


def products(halves, right, prod):
    chunk = 512
    rhs = right[...]
    for n, (ref, begin) in enumerate(halves):
        for first in range(0, HALF, chunk):
            prod[pl.ds(n * HALF + first, chunk), :] = jnp.dot(
                ref[pl.ds(begin + first, chunk), :], rhs, preferred_element_type=jnp.float32
            )


def gather(left_at, right_at, kept, owner, prod, slot_of):
    total = 0
    for b in range(RCAP):
        at = right_at(b)
        j = at & (NC - 1)

        def meet(a, total, b=b, j=j):
            target = (left_at(a) & (MR - 1)) * NC + j
            code = a * RCAP + b
            wanted = kept[target] >= 0
            held = owner[target]
            fresh = jnp.logical_and(wanted, held == 0)

            @pl.when(fresh)
            def _():
                owner[target] = code + 1
                slot_of[total] = code * TILES + target

            @pl.when(jnp.logical_and(wanted, held > 0))
            def _():
                rows, cols = piece(held - 1)
                more_rows, more_cols = piece(code)
                prod[rows, cols] += prod[more_rows, more_cols]

            return total + fresh.astype(jnp.int32)

        k = at >> 3
        total = lax.fori_loop(left_at(LCAP + k), left_at(LCAP + 1 + k), meet, total)
    return total


def write(total, value, slot_of, stage, out, sems):
    def copy_out(slot, target):
        return pltpu.make_async_copy(
            stage.at[slot], block_of(out, target >> 3, target & (NC - 1)), sems.at[slot]
        )

    def send(slot, carry):
        entry = slot_of[slot]
        target = entry & (TILES - 1)
        stage[slot] = value(entry >> 8, target).astype(jnp.bfloat16)
        copy_out(slot, target).start()
        return carry

    def drain(slot, carry):
        copy_out(slot, slot_of[slot] & (TILES - 1)).wait()
        return carry

    lax.fori_loop(0, total, send, 0)
    lax.fori_loop(0, total, drain, 0)


def choose(flag, first, second, held):
    @pl.when(flag == 0)
    def _():
        held[...] = first[pl.ds(0, BLK), :]

    @pl.when(flag != 0)
    def _():
        held[...] = second[pl.ds(0, BLK), :]


def first_kernel(
    keep, left, r0, r1, zero, out, prod, table,
    right, stage, meta_v, meta, slot_of, meta_sem, out_sems,
):
    del zero
    odd = lax.rem(lax.axis_index("row"), 2)
    line = lax.broadcasted_iota(jnp.int32, (META, BLK), 0)
    rows = left[pl.ds(HALF, META), :].astype(jnp.float32)
    for n, ref in enumerate((r0, r1)):
        right_row = ref[pl.ds(BLK, META), pl.ds(0, BLK)].astype(jnp.float32)
        rows = jnp.where(line == 1 + n, right_row, rows)
    meta_v[...] = rows.astype(jnp.int32)
    meta_copy = pltpu.make_async_copy(meta_v, meta, meta_sem)
    meta_copy.start()
    for at in range(TILES):
        table[at] = jnp.minimum(keep[at // NC, at % NC], 1) - 1
    choose(odd, r0, r1, right)
    products(((left, 0), (left, HALF + META)), right, prod)
    meta_copy.wait()
    total = gather(
        lambda a: meta[0, a],
        lambda b: meta[1 + odd, b],
        table,
        table,
        prod,
        slot_of,
    )

    for b in range(RCAP):
        table[TILES + b] = meta[2 - odd, b]

    def value(code, target):
        rows, cols = piece(code)
        return prod[rows, cols]

    write(total, value, slot_of, stage, out, out_sems)


def first(keep, left, r0, r1, zero):
    return pl.pallas_call(
        first_kernel,
        out_shape=(
            jax.ShapeDtypeStruct(zero.shape, zero.dtype),
            jax.ShapeDtypeStruct((LROWS, RCAP * BLK), jnp.float32),
            jax.ShapeDtypeStruct((TILES + BLK,), jnp.int32),
        ),
        in_specs=[spec(pltpu.SMEM)] + [spec(pltpu.VMEM)] * 3 + [spec(pltpu.HBM)],
        out_specs=[spec(pltpu.HBM), spec(pltpu.VMEM), spec(pltpu.SMEM)],
        scratch_shapes=[
            pltpu.VMEM((BLK, RCAP * BLK), jnp.bfloat16),
            pltpu.VMEM((PAIRS, BLK, BLK), jnp.bfloat16),
            pltpu.VMEM((META, BLK), jnp.int32),
            pltpu.SMEM((META, BLK), jnp.int32),
            pltpu.SMEM((PAIRS,), jnp.int32),
            pltpu.SemaphoreType.DMA,
            pltpu.SemaphoreType.DMA((PAIRS,)),
        ],
        input_output_aliases={4: 0},
        compiler_params=pltpu.CompilerParams(vmem_limit_bytes=32 << 20),
        cost_estimate=pl.CostEstimate(
            flops=10**10, bytes_accessed=14 << 20, transcendentals=0
        ),
        name="first",
    )(keep, left, r0, r1, zero)


def last_kernel(
    table_in, left, more, r0, r1, before, zero, out,
    table, table_sem, right, prod, stage, meta_v, meta, owner, slot_of, meta_sem, out_sems,
):
    del zero
    table_copy = pltpu.make_async_copy(table_in, table, table_sem)
    table_copy.start()
    odd = lax.rem(lax.axis_index("row"), 2)
    meta_v[...] = left[pl.ds(HALF, META), :].astype(jnp.float32).astype(jnp.int32)
    meta_copy = pltpu.make_async_copy(meta_v, meta, meta_sem)
    meta_copy.start()
    for at in range(TILES):
        owner[at] = 0
    choose(odd, r1, r0, right)
    products(((left, 0), (more, 0)), right, prod)
    meta_copy.wait()
    table_copy.wait()
    total = gather(
        lambda a: meta[0, a],
        lambda b: table[TILES + b],
        table,
        owner,
        prod,
        slot_of,
    )

    def value(code, target):
        rows, cols = piece(code)
        fresh = prod[rows, cols]
        held = table[target]
        old_rows, old_cols = piece(jnp.maximum(held - 1, 0))
        return jnp.where(held > 0, fresh + before[old_rows, old_cols], fresh)

    write(total, value, slot_of, stage, out, out_sems)


def last(table, left, more, r0, r1, before, out):
    return pl.pallas_call(
        last_kernel,
        out_shape=jax.ShapeDtypeStruct(out.shape, out.dtype),
        in_specs=[spec(pl.ANY)] + [spec(pltpu.VMEM)] * 5 + [spec(pltpu.HBM)],
        out_specs=spec(pltpu.HBM),
        scratch_shapes=[
            pltpu.SMEM(table.shape, jnp.int32),
            pltpu.SemaphoreType.DMA,
            pltpu.VMEM((BLK, RCAP * BLK), jnp.bfloat16),
            pltpu.VMEM((LROWS, RCAP * BLK), jnp.float32),
            pltpu.VMEM((PAIRS, BLK, BLK), jnp.bfloat16),
            pltpu.VMEM((META, BLK), jnp.int32),
            pltpu.SMEM((META, BLK), jnp.int32),
            pltpu.SMEM((TILES,), jnp.int32),
            pltpu.SMEM((PAIRS,), jnp.int32),
            pltpu.SemaphoreType.DMA,
            pltpu.SemaphoreType.DMA((PAIRS,)),
        ],
        input_output_aliases={6: 0},
        compiler_params=pltpu.CompilerParams(vmem_limit_bytes=32 << 20),
        cost_estimate=pl.CostEstimate(
            flops=2 * PAIRS * BLK**3, bytes_accessed=4 << 20, transcendentals=0
        ),
        name="last",
    )(table, left, more, r0, r1, before, out)


def detour(r, c, cols_n, group):
    core, chip = c % group, c // group
    z, x = chip // 2, chip % 2
    depth = cols_n // group // 2
    step = (r + r % 2) // 2 % depth
    source = (chip + r + 1 - r % 2) % (cols_n // group)
    place = source // 2
    if step == 0:
        place = z
    elif 2 * step != depth and 2 * (place - z) % (2 * depth) == depth:
        place = (place + step) % depth
    return source * group + core, (place * 2 + x) * group + core


def on_device(rows_n, cols_n, left_matrix, left_pattern, right_matrix, right_pattern, keep_mask):
    group = cols_n // rows_n

    def send(value, pairs):
        pairs = [(a[0] * cols_n + a[1], b[0] * cols_n + b[1]) for a, b in pairs]
        return lax.ppermute(value, ("row", "col"), pairs)

    devices = [(r, c) for r in range(rows_n) for c in range(cols_n)]

    def moved(value, target):
        pairs = []
        for r, c in devices:
            to_r, to_c = target(r, c)
            pairs.append(((r, c), (to_r % rows_n, to_c % cols_n)))
        return send(value, pairs)

    whole, half = pack_left(left_pattern, left_matrix)
    even = moved(whole, lambda r, c: (r, c - group * (r + r % 2)))
    roads = {at: detour(*at, cols_n, group) for at in devices}
    between = send(half, [((r, roads[r, c][0]), (r, roads[r, c][1])) for r, c in devices])
    rpack = pack_right(right_pattern, right_matrix, whole)
    r0 = moved(rpack, lambda r, c: (r - c // group, c))
    r1 = moved(rpack, lambda r, c: (r - c // group - 1, c))
    zero = blank(rpack, (left_matrix.shape[0], right_matrix.shape[1]))
    part = lax.slice_in_dim(even, 0, HALF + META)
    part, between = lax.optimization_barrier((part, between))
    passed = moved(part, lambda r, c: (r, c + group * (2 * (r % 2) - 1)))
    more = send(between, [((r, roads[r, c][1]), (r, c)) for r, c in devices])
    out, before, table = first(keep_mask, even, r0, r1, zero)
    return last(table, passed, more, r0, r1, before, out)


def solution(mesh):
    part = P("row", "col")
    return jax.shard_map(
        functools.partial(on_device, mesh.shape["row"], mesh.shape["col"]),
        mesh=mesh,
        in_specs=(part,) * 5,
        out_specs=part,
        check_vma=False,
    )
```

```python
import functools

import jax
import jax.numpy as jnp
from jax import lax
from jax.experimental import pallas as pl
from jax.experimental.pallas import tpu as pltpu
from jax.sharding import PartitionSpec as P

BLK = 128
MR = 32
KS = 4
NC = 8
LCAP = 16
RCAP = 4
META = 16
LROWS = LCAP * BLK
ACAP = 6
HALF = ACAP * BLK
REST = LROWS - HALF
PAIRS = LCAP * RCAP
TILES = MR * NC
ZROWS = 256
NOTES = TILES + 64


def block_of(ref, block_row, block_col):
    return ref.at[
        pl.ds(pl.multiple_of(block_row * BLK, BLK), BLK),
        pl.ds(pl.multiple_of(block_col * BLK, BLK), BLK),
    ]


def spec(space):
    return pl.BlockSpec(memory_space=space)


def pack_left_kernel(pattern, left, out, more, pos, meta, sems):
    count = 0
    starts = []
    for k in range(KS):
        starts.append(count)
        for i in range(MR):
            pos[count] = k * MR + i
            count = count + pattern[k, i]
    starts.append(count)
    copies = []
    for a in range(LCAP):
        at = pos[a]
        block = block_of(left, at & (MR - 1), at >> 5)
        first_row = a * BLK if a * BLK < HALF else a * BLK + META
        copies.append(pltpu.make_async_copy(block, out.at[pl.ds(first_row, BLK), :], sems.at[a]))
        copies[-1].start()
        if a * BLK >= HALF:
            copies.append(
                pltpu.make_async_copy(
                    block, more.at[pl.ds(a * BLK - HALF, BLK), :], sems.at[LCAP + a - ACAP]
                )
            )
            copies[-1].start()
    lane = lax.broadcasted_iota(jnp.int32, (META, BLK), 1)
    row = jnp.zeros((META, BLK), jnp.int32)
    for a in range(LCAP):
        row = jnp.where(lane == a, pos[a], row)
    for k in range(KS + 1):
        row = jnp.where(lane == LCAP + k, starts[k], row)
    meta[...] = row.astype(jnp.float32).astype(jnp.bfloat16)
    copies.append(pltpu.make_async_copy(meta, out.at[pl.ds(HALF, META), :], sems.at[2 * LCAP - ACAP]))
    copies[-1].start()
    for copy in copies:
        copy.wait()


def pack_left(pattern, left):
    return pl.pallas_call(
        pack_left_kernel,
        out_shape=(
            jax.ShapeDtypeStruct((LROWS + META, BLK), jnp.bfloat16),
            jax.ShapeDtypeStruct((REST, BLK), jnp.bfloat16),
        ),
        in_specs=[spec(pltpu.SMEM), spec(pltpu.HBM)],
        out_specs=[spec(pl.ANY)] * 2,
        scratch_shapes=[
            pltpu.SMEM((LCAP + 1,), jnp.int32),
            pltpu.VMEM((META, BLK), jnp.bfloat16),
            pltpu.SemaphoreType.DMA((2 * LCAP - ACAP + 1,)),
        ],
        compiler_params=pltpu.CompilerParams(vmem_limit_bytes=52 << 20),
        cost_estimate=pl.CostEstimate(flops=0, bytes_accessed=2 << 20, transcendentals=0),
        name="pack_left",
    )(pattern.T, left)


def pack_right_kernel(pattern, right, after, out, pos, meta, sems):
    del after
    part = lax.rem(lax.axis_index("col"), 2)
    count = 0
    for k in range(KS):
        for j in range(NC):
            pos[count] = k * NC + j
            count = count + pattern[part * KS + k, j]
    copies = []
    for b in range(RCAP):
        at = pos[b]
        copies.append(
            pltpu.make_async_copy(
                block_of(right, part * KS + (at >> 3), at & (NC - 1)),
                out.at[pl.ds(0, BLK), pl.ds(b * BLK, BLK)],
                sems.at[b],
            )
        )
        copies[-1].start()
    lane = lax.broadcasted_iota(jnp.int32, (META, RCAP * BLK), 1)
    row = jnp.zeros((META, RCAP * BLK), jnp.int32)
    for b in range(RCAP):
        row = jnp.where(lane == b, pos[b], row)
    meta[...] = row.astype(jnp.float32).astype(jnp.bfloat16)
    copies.append(pltpu.make_async_copy(meta, out.at[pl.ds(BLK, META), :], sems.at[RCAP]))
    copies[-1].start()
    for copy in copies:
        copy.wait()


def pack_right(pattern, right, after):
    return pl.pallas_call(
        pack_right_kernel,
        out_shape=jax.ShapeDtypeStruct((BLK + META, RCAP * BLK), jnp.bfloat16),
        in_specs=[spec(pltpu.SMEM), spec(pltpu.HBM), spec(pl.ANY)],
        out_specs=spec(pl.ANY),
        scratch_shapes=[
            pltpu.SMEM((RCAP + 1,), jnp.int32),
            pltpu.VMEM((META, RCAP * BLK), jnp.bfloat16),
            pltpu.SemaphoreType.DMA((RCAP + 1,)),
        ],
        compiler_params=pltpu.CompilerParams(vmem_limit_bytes=52 << 20),
        cost_estimate=pl.CostEstimate(flops=0, bytes_accessed=1 << 20, transcendentals=0),
        name="pack_right",
    )(pattern, right, after)


def piece(code):
    return (
        pl.ds(pl.multiple_of((code >> 2) * BLK, BLK), BLK),
        pl.ds(pl.multiple_of((code & 3) * BLK, BLK), BLK),
    )


def products(left, more, begin, right, prod):
    chunk = 256
    rhs = right[...]
    for ref, at, place, size in ((left, 0, 0, HALF), (more, begin, HALF, REST)):
        for first in range(0, size, chunk):
            prod[pl.ds(place + first, chunk), :] = jnp.dot(
                ref[pl.ds(at + first, chunk), :], rhs, preferred_element_type=jnp.float32
            )


def gather(left_at, right_at, kept, owner, prod, slot_of):
    total = 0
    for b in range(RCAP):
        at = right_at(b)
        j = at & (NC - 1)

        def meet(a, total, b=b, j=j):
            target = (left_at(a) & (MR - 1)) * NC + j
            code = a * RCAP + b
            wanted = kept[target] >= 0
            held = owner[target]
            fresh = jnp.logical_and(wanted, held == 0)

            @pl.when(fresh)
            def _():
                owner[target] = code + 1
                slot_of[total] = code * TILES + target

            @pl.when(jnp.logical_and(wanted, held > 0))
            def _():
                rows, cols = piece(held - 1)
                more_rows, more_cols = piece(code)
                prod[rows, cols] += prod[more_rows, more_cols]

            return total + fresh.astype(jnp.int32)

        k = at >> 3
        total = lax.fori_loop(left_at(LCAP + k), left_at(LCAP + 1 + k), meet, total)
    return total


def choose(flag, first, second, held):
    @pl.when(flag == 0)
    def _():
        held[...] = first[pl.ds(0, BLK), :]

    @pl.when(flag != 0)
    def _():
        held[...] = second[pl.ds(0, BLK), :]


def first_kernel(
    keep, left, r0, r1, out, prod, table,
    zero, zero_sems, right, meta_v, meta, slot_of, meta_sem,
):
    zero[...] = jnp.zeros_like(zero)
    clears = [
        pltpu.make_async_copy(zero, out.at[pl.ds(n * ZROWS, ZROWS), :], zero_sems.at[n])
        for n in range(out.shape[0] // ZROWS)
    ]
    for copy in clears:
        copy.start()
    odd = lax.rem(lax.axis_index("row"), 2)
    line = lax.broadcasted_iota(jnp.int32, (META, BLK), 0)
    rows = left[pl.ds(HALF, META), :].astype(jnp.float32)
    for n, ref in enumerate((r0, r1)):
        right_row = ref[pl.ds(BLK, META), pl.ds(0, BLK)].astype(jnp.float32)
        rows = jnp.where(line == 1 + n, right_row, rows)
    meta_v[...] = rows.astype(jnp.int32)
    meta_copy = pltpu.make_async_copy(meta_v, meta, meta_sem)
    meta_copy.start()
    for at in range(TILES):
        table[at] = jnp.minimum(keep[at // NC, at % NC], 1) - 1
    choose(odd, r0, r1, right)
    products(left, left, HALF + META, right, prod)
    meta_copy.wait()
    total = gather(
        lambda a: meta[0, a],
        lambda b: meta[1 + odd, b],
        table,
        table,
        prod,
        slot_of,
    )

    for b in range(RCAP):
        table[TILES + b] = meta[2 - odd, b]
    table[TILES + RCAP] = total

    def note(slot, carry):
        table[NOTES + slot] = slot_of[slot]
        return carry

    lax.fori_loop(0, total, note, 0)
    for copy in clears:
        copy.wait()


def first(keep, left, r0, r1):
    return pl.pallas_call(
        first_kernel,
        out_shape=(
            jax.ShapeDtypeStruct((MR * BLK, NC * BLK), jnp.bfloat16),
            jax.ShapeDtypeStruct((LROWS, RCAP * BLK), jnp.float32),
            jax.ShapeDtypeStruct((NOTES + PAIRS,), jnp.int32),
        ),
        in_specs=[spec(pltpu.SMEM)] + [spec(pltpu.VMEM)] * 3,
        out_specs=[spec(pltpu.HBM), spec(pltpu.VMEM), spec(pltpu.SMEM)],
        scratch_shapes=[
            pltpu.VMEM((ZROWS, NC * BLK), jnp.bfloat16),
            pltpu.SemaphoreType.DMA((MR * BLK // ZROWS,)),
            pltpu.VMEM((BLK, RCAP * BLK), jnp.bfloat16),
            pltpu.VMEM((META, BLK), jnp.int32),
            pltpu.SMEM((META, BLK), jnp.int32),
            pltpu.SMEM((PAIRS,), jnp.int32),
            pltpu.SemaphoreType.DMA,
        ],
        compiler_params=pltpu.CompilerParams(vmem_limit_bytes=32 << 20),
        cost_estimate=pl.CostEstimate(
            flops=10**10, bytes_accessed=14 << 20, transcendentals=0
        ),
        name="first",
    )(keep, left, r0, r1)


def last_kernel(
    table_in, left, more, r0, r1, before, zero, out,
    table, table_sem, right, prod, stage, meta_v, meta, owner, slot_of, meta_sem, out_sems,
):
    del zero
    table_copy = pltpu.make_async_copy(table_in, table, table_sem)
    table_copy.start()
    odd = lax.rem(lax.axis_index("row"), 2)
    meta_v[...] = left[pl.ds(HALF, META), :].astype(jnp.float32).astype(jnp.int32)
    meta_copy = pltpu.make_async_copy(meta_v, meta, meta_sem)
    meta_copy.start()
    for at in range(TILES):
        owner[at] = 0
    choose(odd, r1, r0, right)
    products(left, more, 0, right, prod)
    meta_copy.wait()
    table_copy.wait()
    total = gather(
        lambda a: meta[0, a],
        lambda b: table[TILES + b],
        table,
        owner,
        prod,
        slot_of,
    )

    def copy_out(slot, target):
        return pltpu.make_async_copy(
            stage.at[slot], block_of(out, target >> 3, target & (NC - 1)), out_sems.at[slot]
        )

    def send(slot, carry):
        entry = slot_of[slot]
        target = entry & (TILES - 1)
        rows, cols = piece(entry >> 8)
        fresh = prod[rows, cols]
        held = table[target]
        old_rows, old_cols = piece(jnp.maximum(held - 1, 0))
        both = jnp.where(held > 0, fresh + before[old_rows, old_cols], fresh)
        stage[slot] = both.astype(jnp.bfloat16)
        copy_out(slot, target).start()
        return carry

    def send_old(n, slot):
        entry = table[NOTES + n]
        target = entry & (TILES - 1)
        alone = owner[target] == 0

        @pl.when(alone)
        def _():
            rows, cols = piece(entry >> 8)
            slot_of[slot] = entry
            stage[slot] = before[rows, cols].astype(jnp.bfloat16)
            copy_out(slot, target).start()

        return slot + alone.astype(jnp.int32)

    def drain(slot, carry):
        copy_out(slot, slot_of[slot] & (TILES - 1)).wait()
        return carry

    lax.fori_loop(0, total, send, 0)
    slots = lax.fori_loop(0, table[TILES + RCAP], send_old, total)
    lax.fori_loop(0, slots, drain, 0)


def last(table, left, more, r0, r1, before, out):
    return pl.pallas_call(
        last_kernel,
        out_shape=jax.ShapeDtypeStruct(out.shape, out.dtype),
        in_specs=[spec(pl.ANY)] + [spec(pltpu.VMEM)] * 5 + [spec(pltpu.HBM)],
        out_specs=spec(pltpu.HBM),
        scratch_shapes=[
            pltpu.SMEM(table.shape, jnp.int32),
            pltpu.SemaphoreType.DMA,
            pltpu.VMEM((BLK, RCAP * BLK), jnp.bfloat16),
            pltpu.VMEM((LROWS, RCAP * BLK), jnp.float32),
            pltpu.VMEM((2 * PAIRS, BLK, BLK), jnp.bfloat16),
            pltpu.VMEM((META, BLK), jnp.int32),
            pltpu.SMEM((META, BLK), jnp.int32),
            pltpu.SMEM((TILES,), jnp.int32),
            pltpu.SMEM((2 * PAIRS,), jnp.int32),
            pltpu.SemaphoreType.DMA,
            pltpu.SemaphoreType.DMA((2 * PAIRS,)),
        ],
        input_output_aliases={6: 0},
        compiler_params=pltpu.CompilerParams(vmem_limit_bytes=32 << 20),
        cost_estimate=pl.CostEstimate(
            flops=2 * PAIRS * BLK**3, bytes_accessed=4 << 20, transcendentals=0
        ),
        name="last",
    )(table, left, more, r0, r1, before, out)


def detour(r, c, cols_n, group):
    core, chip = c % group, c // group
    z, x = chip // 2, chip % 2
    depth = cols_n // group // 2
    step = (r + r % 2) // 2 % depth
    source = (chip + r + 1 - r % 2) % (cols_n // group)
    place = source // 2
    if step == 0:
        place = z
    elif 2 * step != depth and 2 * (place - z) % (2 * depth) == depth:
        place = (place + step) % depth
    return source * group + core, (place * 2 + x) * group + core


def on_device(rows_n, cols_n, left_matrix, left_pattern, right_matrix, right_pattern, keep_mask):
    group = cols_n // rows_n

    def send(value, pairs):
        pairs = [(a[0] * cols_n + a[1], b[0] * cols_n + b[1]) for a, b in pairs]
        return lax.ppermute(value, ("row", "col"), pairs)

    devices = [(r, c) for r in range(rows_n) for c in range(cols_n)]

    def moved(value, target):
        pairs = []
        for r, c in devices:
            to_r, to_c = target(r, c)
            pairs.append(((r, c), (to_r % rows_n, to_c % cols_n)))
        return send(value, pairs)

    whole, half = pack_left(left_pattern, left_matrix)
    even = moved(whole, lambda r, c: (r, c - group * (r + r % 2)))
    roads = {at: detour(*at, cols_n, group) for at in devices}
    between = send(half, [((r, roads[r, c][0]), (r, roads[r, c][1])) for r, c in devices])
    rpack = pack_right(right_pattern, right_matrix, whole)
    r0 = moved(rpack, lambda r, c: (r - c // group, c))
    r1 = moved(rpack, lambda r, c: (r - c // group - 1, c))
    passed = moved(
        lax.slice_in_dim(even, 0, HALF + META),
        lambda r, c: (r, c + group * (2 * (r % 2) - 1)),
    )
    more = send(between, [((r, roads[r, c][1]), (r, c)) for r, c in devices])
    out, before, table = first(keep_mask, even, r0, r1)
    return last(table, passed, more, r0, r1, before, out)


def solution(mesh):
    part = P("row", "col")
    return jax.shard_map(
        functools.partial(on_device, mesh.shape["row"], mesh.shape["col"]),
        mesh=mesh,
        in_specs=(part,) * 5,
        out_specs=part,
        check_vma=False,
    )
```

```python
import functools

import jax
import jax.numpy as jnp
from jax import lax
from jax.experimental import pallas as pl
from jax.experimental.pallas import tpu as pltpu
from jax.sharding import PartitionSpec as P

BLK = 128
MR = 32
KS = 4
NC = 8
LCAP = 16
RCAP = 4
META = 16
LROWS = LCAP * BLK
ACAP = 6
HALF = ACAP * BLK
REST = LROWS - HALF
PAIRS = LCAP * RCAP
TILES = MR * NC
NOTES = TILES + 64


def block_of(ref, block_row, block_col):
    return ref.at[
        pl.ds(pl.multiple_of(block_row * BLK, BLK), BLK),
        pl.ds(pl.multiple_of(block_col * BLK, BLK), BLK),
    ]


def spec(space):
    return pl.BlockSpec(memory_space=space)


def pack_left_kernel(pattern, left, out, more, pos, meta, sems):
    count = 0
    starts = []
    for k in range(KS):
        starts.append(count)
        for i in range(MR):
            pos[count] = k * MR + i
            count = count + pattern[k, i]
    starts.append(count)
    copies = []
    for a in range(LCAP):
        at = pos[a]
        block = block_of(left, at & (MR - 1), at >> 5)
        first_row = a * BLK if a * BLK < HALF else a * BLK + META
        copies.append(pltpu.make_async_copy(block, out.at[pl.ds(first_row, BLK), :], sems.at[a]))
        copies[-1].start()
        if a * BLK >= HALF:
            copies.append(
                pltpu.make_async_copy(
                    block, more.at[pl.ds(a * BLK - HALF, BLK), :], sems.at[LCAP + a - ACAP]
                )
            )
            copies[-1].start()
    lane = lax.broadcasted_iota(jnp.int32, (META, BLK), 1)
    row = jnp.zeros((META, BLK), jnp.int32)
    for a in range(LCAP):
        row = jnp.where(lane == a, pos[a], row)
    for k in range(KS + 1):
        row = jnp.where(lane == LCAP + k, starts[k], row)
    meta[...] = row.astype(jnp.float32).astype(jnp.bfloat16)
    copies.append(pltpu.make_async_copy(meta, out.at[pl.ds(HALF, META), :], sems.at[2 * LCAP - ACAP]))
    copies[-1].start()
    for copy in copies:
        copy.wait()


def pack_left(pattern, left):
    return pl.pallas_call(
        pack_left_kernel,
        out_shape=(
            jax.ShapeDtypeStruct((LROWS + META, BLK), jnp.bfloat16),
            jax.ShapeDtypeStruct((REST, BLK), jnp.bfloat16),
        ),
        in_specs=[spec(pltpu.SMEM), spec(pltpu.HBM)],
        out_specs=[spec(pl.ANY)] * 2,
        scratch_shapes=[
            pltpu.SMEM((LCAP + 1,), jnp.int32),
            pltpu.VMEM((META, BLK), jnp.bfloat16),
            pltpu.SemaphoreType.DMA((2 * LCAP - ACAP + 1,)),
        ],
        compiler_params=pltpu.CompilerParams(vmem_limit_bytes=52 << 20),
        cost_estimate=pl.CostEstimate(flops=0, bytes_accessed=2 << 20, transcendentals=0),
        name="pack_left",
    )(pattern.T, left)


def pack_right_kernel(pattern, right, after, out, pos, meta, sems):
    del after
    part = lax.rem(lax.axis_index("col"), 2)
    count = 0
    for k in range(KS):
        for j in range(NC):
            pos[count] = k * NC + j
            count = count + pattern[part * KS + k, j]
    copies = []
    for b in range(RCAP):
        at = pos[b]
        copies.append(
            pltpu.make_async_copy(
                block_of(right, part * KS + (at >> 3), at & (NC - 1)),
                out.at[pl.ds(0, BLK), pl.ds(b * BLK, BLK)],
                sems.at[b],
            )
        )
        copies[-1].start()
    lane = lax.broadcasted_iota(jnp.int32, (META, RCAP * BLK), 1)
    row = jnp.zeros((META, RCAP * BLK), jnp.int32)
    for b in range(RCAP):
        row = jnp.where(lane == b, pos[b], row)
    meta[...] = row.astype(jnp.float32).astype(jnp.bfloat16)
    copies.append(pltpu.make_async_copy(meta, out.at[pl.ds(BLK, META), :], sems.at[RCAP]))
    copies[-1].start()
    for copy in copies:
        copy.wait()


def pack_right(pattern, right, after):
    return pl.pallas_call(
        pack_right_kernel,
        out_shape=jax.ShapeDtypeStruct((BLK + META, RCAP * BLK), jnp.bfloat16),
        in_specs=[spec(pltpu.SMEM), spec(pltpu.HBM), spec(pl.ANY)],
        out_specs=spec(pl.ANY),
        scratch_shapes=[
            pltpu.SMEM((RCAP + 1,), jnp.int32),
            pltpu.VMEM((META, RCAP * BLK), jnp.bfloat16),
            pltpu.SemaphoreType.DMA((RCAP + 1,)),
        ],
        compiler_params=pltpu.CompilerParams(vmem_limit_bytes=52 << 20),
        cost_estimate=pl.CostEstimate(flops=0, bytes_accessed=1 << 20, transcendentals=0),
        name="pack_right",
    )(pattern, right, after)


def blank_kernel(after, out, zero, sems):
    del after
    zero[...] = jnp.zeros_like(zero)
    rows = zero.shape[0]
    copies = [
        pltpu.make_async_copy(zero, out.at[pl.ds(n * rows, rows), :], sems.at[n])
        for n in range(out.shape[0] // rows)
    ]
    for copy in copies:
        copy.start()
    for copy in copies:
        copy.wait()


def blank(after, shape):
    rows = 256
    return pl.pallas_call(
        blank_kernel,
        out_shape=jax.ShapeDtypeStruct(shape, jnp.bfloat16),
        in_specs=[spec(pl.ANY)],
        out_specs=spec(pltpu.HBM),
        scratch_shapes=[
            pltpu.VMEM((rows, shape[1]), jnp.bfloat16),
            pltpu.SemaphoreType.DMA((shape[0] // rows,)),
        ],
        cost_estimate=pl.CostEstimate(
            flops=10**10, bytes_accessed=2 * shape[0] * shape[1], transcendentals=0
        ),
        name="blank",
    )(after)


def piece(code):
    return (
        pl.ds(pl.multiple_of((code >> 2) * BLK, BLK), BLK),
        pl.ds(pl.multiple_of((code & 3) * BLK, BLK), BLK),
    )


def products(left, more, begin, right, prod):
    chunk = 256
    rhs = right[...]
    for ref, at, place, size in ((left, 0, 0, HALF), (more, begin, HALF, REST)):
        for first in range(0, size, chunk):
            prod[pl.ds(place + first, chunk), :] = jnp.dot(
                ref[pl.ds(at + first, chunk), :], rhs, preferred_element_type=jnp.float32
            )


def gather(left_at, right_at, kept, owner, prod, slot_of):
    total = 0
    for b in range(RCAP):
        at = right_at(b)
        j = at & (NC - 1)

        def meet(a, total, b=b, j=j):
            target = (left_at(a) & (MR - 1)) * NC + j
            code = a * RCAP + b
            wanted = kept[target] >= 0
            held = owner[target]
            fresh = jnp.logical_and(wanted, held == 0)

            @pl.when(fresh)
            def _():
                owner[target] = code + 1
                slot_of[total] = code * TILES + target

            @pl.when(jnp.logical_and(wanted, held > 0))
            def _():
                rows, cols = piece(held - 1)
                more_rows, more_cols = piece(code)
                prod[rows, cols] += prod[more_rows, more_cols]

            return total + fresh.astype(jnp.int32)

        k = at >> 3
        total = lax.fori_loop(left_at(LCAP + k), left_at(LCAP + 1 + k), meet, total)
    return total


def choose(flag, first, second, held):
    @pl.when(flag == 0)
    def _():
        held[...] = first[pl.ds(0, BLK), :]

    @pl.when(flag != 0)
    def _():
        held[...] = second[pl.ds(0, BLK), :]


def first_kernel(
    keep, left, r0, r1, prod, table,
    right, meta_v, meta, slot_of, meta_sem,
):
    odd = lax.rem(lax.axis_index("row"), 2)
    line = lax.broadcasted_iota(jnp.int32, (META, BLK), 0)
    rows = left[pl.ds(HALF, META), :].astype(jnp.float32)
    for n, ref in enumerate((r0, r1)):
        right_row = ref[pl.ds(BLK, META), pl.ds(0, BLK)].astype(jnp.float32)
        rows = jnp.where(line == 1 + n, right_row, rows)
    meta_v[...] = rows.astype(jnp.int32)
    meta_copy = pltpu.make_async_copy(meta_v, meta, meta_sem)
    meta_copy.start()
    for at in range(TILES):
        table[at] = jnp.minimum(keep[at // NC, at % NC], 1) - 1
    choose(odd, r0, r1, right)
    products(left, left, HALF + META, right, prod)
    meta_copy.wait()
    total = gather(
        lambda a: meta[0, a],
        lambda b: meta[1 + odd, b],
        table,
        table,
        prod,
        slot_of,
    )

    for b in range(RCAP):
        table[TILES + b] = meta[2 - odd, b]
    table[TILES + RCAP] = total

    def note(slot, carry):
        table[NOTES + slot] = slot_of[slot]
        return carry

    lax.fori_loop(0, total, note, 0)


def first(keep, left, r0, r1):
    return pl.pallas_call(
        first_kernel,
        out_shape=(
            jax.ShapeDtypeStruct((LROWS, RCAP * BLK), jnp.float32),
            jax.ShapeDtypeStruct((NOTES + PAIRS,), jnp.int32),
        ),
        in_specs=[spec(pltpu.SMEM)] + [spec(pltpu.VMEM)] * 3,
        out_specs=[spec(pltpu.VMEM), spec(pltpu.SMEM)],
        scratch_shapes=[
            pltpu.VMEM((BLK, RCAP * BLK), jnp.bfloat16),
            pltpu.VMEM((META, BLK), jnp.int32),
            pltpu.SMEM((META, BLK), jnp.int32),
            pltpu.SMEM((PAIRS,), jnp.int32),
            pltpu.SemaphoreType.DMA,
        ],
        compiler_params=pltpu.CompilerParams(vmem_limit_bytes=32 << 20),
        cost_estimate=pl.CostEstimate(
            flops=2 * PAIRS * BLK**3, bytes_accessed=14 << 20, transcendentals=0
        ),
        name="first",
    )(keep, left, r0, r1)


def last_kernel(
    table_in, left, more, r0, r1, before, zero, out,
    table, table_sem, right, prod, stage, meta_v, meta, owner, slot_of, meta_sem, out_sems,
):
    del zero
    table_copy = pltpu.make_async_copy(table_in, table, table_sem)
    table_copy.start()
    odd = lax.rem(lax.axis_index("row"), 2)
    meta_v[...] = left[pl.ds(HALF, META), :].astype(jnp.float32).astype(jnp.int32)
    meta_copy = pltpu.make_async_copy(meta_v, meta, meta_sem)
    meta_copy.start()
    for at in range(TILES):
        owner[at] = 0
    choose(odd, r1, r0, right)
    products(left, more, 0, right, prod)
    meta_copy.wait()
    table_copy.wait()
    total = gather(
        lambda a: meta[0, a],
        lambda b: table[TILES + b],
        table,
        owner,
        prod,
        slot_of,
    )

    def copy_out(slot, target):
        return pltpu.make_async_copy(
            stage.at[slot], block_of(out, target >> 3, target & (NC - 1)), out_sems.at[slot]
        )

    def send(slot, carry):
        entry = slot_of[slot]
        target = entry & (TILES - 1)
        rows, cols = piece(entry >> 8)
        fresh = prod[rows, cols]
        held = table[target]
        old_rows, old_cols = piece(jnp.maximum(held - 1, 0))
        both = jnp.where(held > 0, fresh + before[old_rows, old_cols], fresh)
        stage[slot] = both.astype(jnp.bfloat16)
        copy_out(slot, target).start()
        return carry

    def send_old(n, slot):
        entry = table[NOTES + n]
        target = entry & (TILES - 1)
        alone = owner[target] == 0

        @pl.when(alone)
        def _():
            rows, cols = piece(entry >> 8)
            slot_of[slot] = entry
            stage[slot] = before[rows, cols].astype(jnp.bfloat16)
            copy_out(slot, target).start()

        return slot + alone.astype(jnp.int32)

    def drain(slot, carry):
        copy_out(slot, slot_of[slot] & (TILES - 1)).wait()
        return carry

    lax.fori_loop(0, total, send, 0)
    slots = lax.fori_loop(0, table[TILES + RCAP], send_old, total)
    lax.fori_loop(0, slots, drain, 0)


def last(table, left, more, r0, r1, before, out):
    return pl.pallas_call(
        last_kernel,
        out_shape=jax.ShapeDtypeStruct(out.shape, out.dtype),
        in_specs=[spec(pl.ANY)] + [spec(pltpu.VMEM)] * 5 + [spec(pltpu.HBM)],
        out_specs=spec(pltpu.HBM),
        scratch_shapes=[
            pltpu.SMEM(table.shape, jnp.int32),
            pltpu.SemaphoreType.DMA,
            pltpu.VMEM((BLK, RCAP * BLK), jnp.bfloat16),
            pltpu.VMEM((LROWS, RCAP * BLK), jnp.float32),
            pltpu.VMEM((2 * PAIRS, BLK, BLK), jnp.bfloat16),
            pltpu.VMEM((META, BLK), jnp.int32),
            pltpu.SMEM((META, BLK), jnp.int32),
            pltpu.SMEM((TILES,), jnp.int32),
            pltpu.SMEM((2 * PAIRS,), jnp.int32),
            pltpu.SemaphoreType.DMA,
            pltpu.SemaphoreType.DMA((2 * PAIRS,)),
        ],
        input_output_aliases={6: 0},
        compiler_params=pltpu.CompilerParams(vmem_limit_bytes=32 << 20),
        cost_estimate=pl.CostEstimate(
            flops=2 * PAIRS * BLK**3, bytes_accessed=4 << 20, transcendentals=0
        ),
        name="last",
    )(table, left, more, r0, r1, before, out)


def detour(r, c, cols_n, group):
    core, chip = c % group, c // group
    z, x = chip // 2, chip % 2
    depth = cols_n // group // 2
    step = (r + r % 2) // 2 % depth
    source = (chip + r + 1 - r % 2) % (cols_n // group)
    place = source // 2
    if step == 0:
        place = z
    elif 2 * step != depth and 2 * (place - z) % (2 * depth) == depth:
        place = (place + step) % depth
    return source * group + core, (place * 2 + x) * group + core


def on_device(rows_n, cols_n, left_matrix, left_pattern, right_matrix, right_pattern, keep_mask):
    group = cols_n // rows_n

    def send(value, pairs):
        pairs = [(a[0] * cols_n + a[1], b[0] * cols_n + b[1]) for a, b in pairs]
        return lax.ppermute(value, ("row", "col"), pairs)

    devices = [(r, c) for r in range(rows_n) for c in range(cols_n)]

    def moved(value, target):
        pairs = []
        for r, c in devices:
            to_r, to_c = target(r, c)
            pairs.append(((r, c), (to_r % rows_n, to_c % cols_n)))
        return send(value, pairs)

    whole, half = pack_left(left_pattern, left_matrix)
    even = moved(whole, lambda r, c: (r, c - group * (r + r % 2)))
    roads = {at: detour(*at, cols_n, group) for at in devices}
    between = send(half, [((r, roads[r, c][0]), (r, roads[r, c][1])) for r, c in devices])
    rpack = pack_right(right_pattern, right_matrix, whole)
    r0 = moved(rpack, lambda r, c: (r - c // group, c))
    r1 = moved(rpack, lambda r, c: (r - c // group - 1, c))
    passed = moved(
        lax.slice_in_dim(even, 0, HALF + META),
        lambda r, c: (r, c + group * (2 * (r % 2) - 1)),
    )
    more = send(between, [((r, roads[r, c][1]), (r, c)) for r, c in devices])
    zero = blank(even, (left_matrix.shape[0], right_matrix.shape[1]))
    before, table = first(keep_mask, even, r0, r1)
    return last(table, passed, more, r0, r1, before, zero)


def solution(mesh):
    part = P("row", "col")
    return jax.shard_map(
        functools.partial(on_device, mesh.shape["row"], mesh.shape["col"]),
        mesh=mesh,
        in_specs=(part,) * 5,
        out_specs=part,
        check_vma=False,
    )
```
